128 devices in a mesh: snd: 8 (over z, core), tile: 16 (over x, y).
Axes of the slice: x: 4, y: 4, z: 4, core: 2. Of those that a mesh axis runs over, the one named last changes fastest.
Arguments:
- level_set: float32 [128, 30720], P('tile'), may hold values from -6 to 6
- tile_home: int32 [128], replicated, may hold values from 0 to 127, as said below
- footprints: int32 [128, 16], P(('snd', 'tile')), may hold values from 0 to 127, as said below
- adjoint_source: bfloat16 [128, 48, 4096], P(('snd', 'tile')), may hold values from -6 to 6
- primal_fields: bfloat16 [128, 3, 48, 4096], P(('snd', 'tile')), may hold values from -6 to 6
Outputs:
- level_grad: float32 [128, 30720], P('tile')
- level_next: float32 [128, 30720], P('tile')
The draws below stay inside these ranges and needn't reach their ends.
Inputs may be any that keep to these rules, and one draw needn't show every extreme that they name: A permutation: tile g is stored in row tile_home[g] of level_set, on index tile_home[g] // 8 of tile. `footprints`: the 16 tiles of one sounding are distinct; for each index of tile, either none or exactly two of them are stored there.
All inputs are finite; a program needn't handle non-finite values. Where the reference program divides by a largest or mean magnitude, that divisor is 1e-20 or more.
Results may differ from the reference program's by a relative error of at most 0.0003.
Values sent between devices are 32-bit elements; how exact they have to be, the bound alone decides.
A program may use at most 64 MiB of HBM per device.

```python
import jax
import jax.numpy as jnp
from jax import lax

TX = 16
DEPTH = 48
FOOT = 4
JACOBI = 8
S_DEV = 1
SOUNDINGS = 128
TILE_DEV = 8
TILES = 128
CELLS_M = 30720
FH = 4096
N_TILE = 16


def layout_tables(key):
    storage = jax.random.permutation(jax.random.fold_in(key, 7), TILES).astype(jnp.int32)
    inverse = jnp.argsort(storage).astype(jnp.int32)
    return (storage, inverse)


def draw_tile_home(key, part):
    return layout_tables(key)[0]


def order_group(group_key):
    return jax.random.permutation(group_key, N_TILE).astype(jnp.int32)


def order_entries(entry_key):
    return jax.random.permutation(entry_key, FOOT * FOOT).astype(jnp.int32)


def draw_footprints(key, part):
    storage, inverse = layout_tables(key)
    pairs = FOOT * FOOT // 2
    group_count = SOUNDINGS // (S_DEV * N_TILE)
    group_keys = jax.random.split(jax.random.fold_in(key, 13), group_count)
    orders = jax.vmap(order_group)(group_keys)
    sounding_group = jnp.arange(SOUNDINGS) // (S_DEV * N_TILE)
    reach = min(pairs - 1, N_TILE - pairs)
    shifts = jax.random.randint(jax.random.fold_in(key, 17), (SOUNDINGS,), 0, reach + 1)
    pair_index = jnp.arange(FOOT * FOOT) // 2
    position = (shifts[:, None] + pair_index[None, :]).astype(jnp.int32)
    owner = jnp.take_along_axis(orders[sounding_group], position, axis=1)
    first_row = jax.random.randint(jax.random.fold_in(key, 19), (SOUNDINGS, pairs), 0, TILE_DEV)
    offset = jax.random.randint(jax.random.fold_in(key, 23), (SOUNDINGS, pairs), 1, TILE_DEV)
    second_row = (first_row + offset) % TILE_DEV
    local_rows = jnp.stack([first_row, second_row], axis=2).reshape(SOUNDINGS, FOOT * FOOT)
    stored = (owner * TILE_DEV + local_rows).astype(jnp.int32)
    placed = jnp.take(inverse, stored, axis=0)
    entry_keys = jax.random.split(jax.random.fold_in(key, 29), SOUNDINGS)
    arrangement = jax.vmap(order_entries)(entry_keys)
    return jnp.take_along_axis(placed, arrangement, axis=1).astype(jnp.int32)


def steps_of(stream_key, extent, cuts, least, high):
    def one(axis_at, blocks):
        steps = jax.random.uniform(jax.random.fold_in(jax.random.fold_in(stream_key, 6), axis_at), (blocks,), jnp.float32, least / len(cuts), high / len(cuts))
        return jnp.repeat(jnp.exp(steps), extent[axis_at] // blocks).reshape((-1,) + (1,) * (len(extent) - axis_at - 1))

    level = one(*cuts[0])
    for cut in cuts[1:]:
        level = level * one(*cut)
    return level


def scatter_about(stream_key, extent, deviation, most, cuts=(), kind=jnp.bfloat16):
    loudness = steps_of(stream_key, extent, cuts, -0.22, 0.18) if cuts else 1.0
    values = jax.random.normal(stream_key, extent, jnp.float32) * deviation * loudness
    return jnp.minimum(jnp.maximum(values, -most), most).astype(kind)


def setup_inputs(seed: int = 0) -> dict:
    splits = jax.random.split(jax.random.key(seed), 6)
    level_set = scatter_about(splits[0], (TILES, CELLS_M), 1.0, 6.0, ((0, 16),), jnp.float32)
    tile_home = draw_tile_home(jax.random.fold_in(splits[5], 71), 0)
    footprints = draw_footprints(jax.random.fold_in(splits[5], 71), 0)
    adjoint_source = scatter_about(splits[3], (SOUNDINGS, DEPTH, FH), 1.0, 6.0, ((0, 128),))
    primal_fields = scatter_about(splits[4], (SOUNDINGS, 3, DEPTH, FH), 1.0, 6.0, ((0, 128),))
    return dict(level_set=level_set, tile_home=tile_home, footprints=footprints, adjoint_source=adjoint_source, primal_fields=primal_fields)


log_low = -1.2
log_span = 2.5
front_width = 0.5
step_size = 0.5


def neighbours(values, mesh_side):
    batch, layers, plane = values.shape
    column = jnp.arange(plane) % mesh_side
    zero_layer = jnp.zeros((batch, 1, plane), jnp.float32)
    result = jnp.concatenate([zero_layer, values[:, :-1]], axis=1) + jnp.concatenate([values[:, 1:], zero_layer], axis=1)
    zero_rows = jnp.zeros((batch, layers, mesh_side), jnp.float32)
    result = result + jnp.concatenate([zero_rows, values[:, :, :-mesh_side]], axis=2)
    result = result + jnp.concatenate([values[:, :, mesh_side:], zero_rows], axis=2)
    zero_col = jnp.zeros((batch, layers, 1), jnp.float32)
    western = jnp.where(column != 0, jnp.concatenate([zero_col, values[:, :, :-1]], axis=2), 0.0)
    eastern = jnp.where(column != mesh_side - 1, jnp.concatenate([values[:, :, 1:], zero_col], axis=2), 0.0)
    return result + western + eastern


def jacobi_solve(source, inverse_diag, mesh_side):
    iterate = jnp.zeros(source.shape, jnp.float32)
    for sweep_index in range(JACOBI):
        iterate = (source + neighbours(iterate, mesh_side)) * inverse_diag
    return iterate


def sensitivity(phi_field, sources, primals, mesh_side):
    smooth = jnp.tanh(phi_field / front_width)
    conduct = jnp.exp(log_low + 0.5 * log_span * (1.0 + smooth))
    slope_term = conduct * (0.5 * log_span / front_width) * (1.0 - smooth * smooth)
    inverse_diag = 1.0 / (6.0 + conduct)
    adjoint_two = jacobi_solve(sources.astype(jnp.float32), inverse_diag, mesh_side)
    adjoint_one = jacobi_solve(conduct * adjoint_two, inverse_diag, mesh_side)
    fields = primals.astype(jnp.float32)
    return -slope_term * (adjoint_two * (fields[:, 2] - fields[:, 1]) + adjoint_one * (fields[:, 1] - fields[:, 0]))


def to_footprint(entries, block_size):
    shaped = entries.reshape(block_size, FOOT, FOOT, DEPTH, TX, TX)
    return shaped.transpose(0, 3, 1, 4, 2, 5).reshape(block_size, DEPTH, FOOT * TX * FOOT * TX)


def to_entries(footprint_field, block_size):
    shaped = footprint_field.reshape(block_size, DEPTH, FOOT, TX, FOOT, TX)
    return shaped.transpose(0, 2, 4, 1, 3, 5).reshape(block_size * FOOT * FOOT, DEPTH * TX * TX)


def reference(level_set, tile_home, footprints, adjoint_source, primal_fields):
    mesh_side = FOOT * TX
    top_cells = DEPTH * TX * TX
    block_count = SOUNDINGS // S_DEV
    tile_lists = footprints.reshape(block_count, S_DEV, FOOT * FOOT)
    sources = adjoint_source.reshape(block_count, S_DEV, DEPTH, mesh_side * mesh_side)
    primals = primal_fields.reshape(block_count, S_DEV, 3, DEPTH, mesh_side * mesh_side)
    top_level = level_set[:, :top_cells]

    def accumulate(summed, pieces):
        tile_ids, block_sources, block_primals = pieces
        stored = jnp.take(tile_home, tile_ids.reshape(-1), axis=0).astype(jnp.int32)
        entries = jnp.take(top_level, stored, axis=0)
        phi_field = to_footprint(entries, S_DEV)
        gradient = to_entries(sensitivity(phi_field, block_sources, block_primals, mesh_side), S_DEV)
        return summed.at[stored].add(gradient), None

    summed, unused = lax.scan(accumulate, jnp.zeros((TILES, top_cells), jnp.float32), (tile_lists, sources, primals))
    full_grad = jnp.concatenate([summed, jnp.zeros((TILES, level_set.shape[1] - top_cells), jnp.float32)], axis=1)
    largest = jnp.max(jnp.abs(full_grad))
    return full_grad, level_set - step_size * full_grad / (largest + 1e-6)
```

```python
import functools

import jax
import jax.numpy as jnp
from jax import lax
from jax.experimental import pallas as pl
from jax.experimental.pallas import tpu as pltpu
from jax.sharding import PartitionSpec as P

MESH = pl.DeviceIdType.MESH

TX = 16
DEPTH = 48
FOOT = 4
JACOBI = 8
NTILE = 16
NSND = 8
TDEV = 8
TILES = NTILE * TDEV
ENTRIES = FOOT * FOOT
TOP = DEPTH * TX * TX
SLAB = TOP // NSND
CHUNKS = SLAB // 128
SROWS = CHUNKS * ENTRIES

log_low = -1.2
log_span = 2.5
front_width = 0.5
step_size = 0.5


def exchange_groups(blocks, lane):
    blocks = list(blocks)
    for bit in range(3):
        shift = TX << bit
        low = (lane & shift) == 0
        for i in range(8):
            if i & (1 << bit):
                continue
            j = i | (1 << bit)
            a, b = blocks[i], blocks[j]
            blocks[i] = jnp.where(low, a, pltpu.roll(b, shift, 1))
            blocks[j] = jnp.where(low, pltpu.roll(a, 128 - shift, 1), b)
    return blocks


def split3(x):
    hi = x.astype(jnp.bfloat16)
    rest = x - hi.astype(jnp.float32)
    mid = rest.astype(jnp.bfloat16)
    lo = (rest - mid.astype(jnp.float32)).astype(jnp.bfloat16)
    return hi, mid, lo


def onehot_dot(onehot, x):
    return sum(jnp.dot(onehot, part, preferred_element_type=jnp.float32) for part in split3(x))


def kernel(
    footprints,
    tile_home,
    level_set,
    adjoint_source,
    primal_fields,
    grad_ref,
    peak_ref,
    src_in,
    prim_in,
    gathered,
    request,
    picked,
    returned,
    source,
    diff21,
    diff10,
    conduct,
    inverse,
    slope,
    va,
    vb,
    adjoint_two,
    outgoing,
    arrived,
    partial,
    owned,
    peaks,
    peaks2,
    local_sem,
    ag_send,
    ag_recv,
    rq_send,
    rq_recv,
    pk_send,
    pk_recv,
    og_send,
    og_recv,
    rs_send,
    rs_recv,
    fin_send,
    fin_recv,
    mp_send,
    mp_recv,
    mc_send,
    mc_recv,
):
    snd = lax.axis_index("snd")
    tile = lax.axis_index("tile")
    x, y = tile // 4, tile % 4
    z, core = snd // 2, snd % 2

    plane = []
    for i in range(1, 16):
        dx, dy = i // 4, i % 4
        to = ((x + dx) % 4) * 4 + (y + dy) % 4
        frm = ((x + 4 - dx) % 4) * 4 + (y + 4 - dy) % 4
        plane.append((i, to, frm))
    column = []
    for i in range(1, 8):
        dz, dc = i // 2, i % 2
        to = ((z + dz) % 4) * 2 + (core + dc) % 2
        frm = ((z + 4 - dz) % 4) * 2 + (core + dc) % 2
        column.append((i, to, frm))

    load_src = pltpu.make_async_copy(adjoint_source, src_in, local_sem.at[0])
    load_prim = pltpu.make_async_copy(primal_fields, prim_in, local_sem.at[1])
    own_cells = level_set.at[:, pl.ds(pl.multiple_of(snd * SLAB, SLAB), SLAB)]
    load_own = pltpu.make_async_copy(own_cells, gathered.at[tile], local_sem.at[2])
    load_own.start()
    load_src.start()
    load_prim.start()

    barrier = pltpu.get_barrier_semaphore()
    for _, to, _ in plane:
        pl.semaphore_signal(barrier, inc=1, device_id=(snd, to), device_id_type=MESH)
    for _, to, _ in column:
        pl.semaphore_signal(barrier, inc=1, device_id=(to, tile), device_id_type=MESH)

    wanted_rows = lax.broadcasted_iota(jnp.int32, (ENTRIES, TILES), 0)
    stored_rows = lax.broadcasted_iota(jnp.int32, (ENTRIES, TILES), 1)
    wanted = jnp.zeros((ENTRIES, TILES), jnp.int32)
    for j in range(ENTRIES):
        wanted = jnp.where(wanted_rows == j, tile_home[footprints[0, j]], wanted)
    mine = pl.ds(pl.multiple_of(snd * ENTRIES, ENTRIES), ENTRIES)
    request[mine, :] = jnp.where(wanted == stored_rows, 1.0, 0.0)

    pl.semaphore_wait(barrier, 22)

    ag, rq = [], []
    load_own.wait()
    for i, to, frm in plane:
        copy = pltpu.make_async_remote_copy(
            gathered.at[tile], gathered.at[tile], ag_send.at[i], ag_recv.at[i], (snd, to), MESH
        )
        copy.start()
        ag.append(copy)
    for i, to, frm in column:
        copy = pltpu.make_async_remote_copy(
            request.at[mine], request.at[mine], rq_send.at[i], rq_recv.at[i], (to, tile), MESH
        )
        copy.start()
        rq.append(copy)

    lane = lax.broadcasted_iota(jnp.int32, (DEPTH, 128), 1)
    left = lane < 64

    def halves(top, bottom):
        return (
            jnp.where(left, top, pltpu.roll(bottom, 64, 1)),
            jnp.where(left, pltpu.roll(top, 64, 1), bottom),
        )

    load_src.wait()
    load_prim.wait()

    def lay_out(rp, carry):
        low = pl.ds(pl.multiple_of(rp * 128, 128), 128)
        high = pl.ds(pl.multiple_of(rp * 128 + 2048, 128), 128)
        even, odd = halves(
            src_in[0, :, low].astype(jnp.float32), src_in[0, :, high].astype(jnp.float32)
        )
        source[2 * rp] = even
        source[2 * rp + 1] = odd
        fields = [
            [prim_in[0, k, :, part].astype(jnp.float32) for part in (low, high)] for k in range(3)
        ]
        even, odd = halves(fields[2][0] - fields[1][0], fields[2][1] - fields[1][1])
        diff21[2 * rp] = even
        diff21[2 * rp + 1] = odd
        even, odd = halves(fields[1][0] - fields[0][0], fields[1][1] - fields[0][1])
        diff10[2 * rp] = even
        diff10[2 * rp + 1] = odd
        return carry

    lax.fori_loop(0, 16, lay_out, 0)

    zeros8 = jnp.zeros((34, 8, 128), jnp.float32)
    for buf in (va, vb):
        buf[:, 0:8, :] = zeros8
        buf[:, 56:64, :] = zeros8

    for copy in rq:
        copy.wait()
    for copy in ag:
        copy.wait()
    onehot = request[...]
    pick = onehot.astype(jnp.bfloat16)
    place = onehot.T.astype(jnp.bfloat16)
    for c in range(CHUNKS):
        cells = gathered[:, :, c * 128 : (c + 1) * 128].reshape(TILES, 128)
        picked[:, c * ENTRIES : (c + 1) * ENTRIES, :] = onehot_dot(pick, cells).reshape(
            NSND, ENTRIES, 128
        )
    slab_rows = pl.ds(pl.multiple_of(snd * SROWS, SROWS), SROWS)
    pk = []
    for i, to, frm in column:
        copy = pltpu.make_async_remote_copy(
            picked.at[to], returned.at[slab_rows], pk_send.at[i], pk_recv.at[i], (to, tile), MESH
        )
        copy.start()
        pk.append(copy)
    returned[slab_rows, :] = picked[snd]
    for copy in pk:
        copy.wait()

    lane8 = lax.broadcasted_iota(jnp.int32, (8, 128), 1)

    def block_rows(step, g):
        db, rest = step // 4, step % 4
        th, b1 = rest // 2, rest % 2
        entry = (2 * (g // 4) + b1) * 4 + g % 4
        start = (db * 16 + th) * ENTRIES + entry
        return pl.ds(start, 8, stride=2 * ENTRIES), pl.multiple_of(db * 8, 8), b1 * 16 + th * 8

    def enter(step, carry):
        blocks = []
        for g in range(8):
            rows, depth, row = block_rows(step, g)
            blocks.append(returned[rows, :])
        for q, phi in enumerate(exchange_groups(blocks, lane8)):
            smooth = jnp.tanh(phi / front_width)
            cond = jnp.exp(log_low + 0.5 * log_span * (1.0 + smooth))
            at = pl.ds(depth, 8)
            inv = 1.0 / (6.0 + cond)
            conduct[row + q, at, :] = cond
            inverse[row + q, at, :] = inv
            slope[row + q, at, :] = (
                cond * (0.5 * log_span / front_width) * (1.0 - smooth * smooth)
            )
            va[row + q + 1, pl.ds(depth + 8, 8), :] = source[row + q, at, :] * inv
        return carry

    lax.fori_loop(0, 24, enter, 0)

    col = lane & 63
    not_first = col != 0
    not_last = col != 63

    def edges(buf):
        buf[0, 8:56, :] = jnp.where(left, 0.0, pltpu.roll(buf[32, 8:56, :], 64, 1))
        buf[33, 8:56, :] = jnp.where(left, pltpu.roll(buf[1, 8:56, :], 64, 1), 0.0)

    def relaxed(now, row, rhs):
        v = now[row + 1, 8:56, :]
        total = now[row + 1, 7:55, :] + now[row + 1, 9:57, :]
        total = total + now[row, 8:56, :] + now[row + 2, 8:56, :]
        total = total + jnp.where(not_first, pltpu.roll(v, 1, 1), 0.0)
        total = total + jnp.where(not_last, pltpu.roll(v, 127, 1), 0.0)
        return (rhs[row] + total) * inverse[row]

    def solve(rhs, last):
        now, later = va, vb
        for sweep in range(1, JACOBI):
            edges(now)
            final = sweep == JACOBI - 1

            def body(row, carry, now=now, later=later, final=final):
                value = relaxed(now, row, rhs)
                if final:
                    last(row, value)
                else:
                    later[row + 1, 8:56, :] = value
                return carry

            lax.fori_loop(0, 32, body, 0)
            now, later = later, now

    def keep_two(row, value):
        adjoint_two[row] = value

    solve(source, keep_two)

    def second(row, carry):
        rhs = conduct[row] * adjoint_two[row]
        source[row] = rhs
        va[row + 1, 8:56, :] = rhs * inverse[row]
        return carry

    lax.fori_loop(0, 32, second, 0)

    def gradient(row, value):
        vb[row + 1, 8:56, :] = -slope[row] * (
            adjoint_two[row] * diff21[row] + value * diff10[row]
        )

    solve(source, gradient)

    def leave(step, carry):
        _, depth, row = block_rows(step, 0)
        blocks = [vb[row + q + 1, pl.ds(depth + 8, 8), :] for q in range(8)]
        for g, block in enumerate(exchange_groups(blocks, lane8)):
            rows, _, _ = block_rows(step, g)
            outgoing[rows, :] = block
        return carry

    lax.fori_loop(0, 24, leave, 0)

    og = []
    for i, to, frm in column:
        rows = pl.ds(pl.multiple_of(to * SROWS, SROWS), SROWS)
        copy = pltpu.make_async_remote_copy(
            outgoing.at[rows], arrived.at[snd], og_send.at[i], og_recv.at[i], (to, tile), MESH
        )
        copy.start()
        og.append(copy)
    arrived[snd] = outgoing[slab_rows, :]
    for copy in og:
        copy.wait()
    for c in range(CHUNKS):
        cells = arrived[:, c * ENTRIES : (c + 1) * ENTRIES, :].reshape(TILES, 128)
        partial[:, :, c * 128 : (c + 1) * 128] = onehot_dot(place, cells).reshape(
            NTILE, TDEV, 128
        )

    rs = []
    for i, to, frm in plane:
        copy = pltpu.make_async_remote_copy(
            partial.at[to], owned.at[tile], rs_send.at[i], rs_recv.at[i], (snd, to), MESH
        )
        copy.start()
        rs.append(copy)
    owned[tile] = partial[tile]
    for copy in rs:
        copy.wait()
    slab = owned[0]
    for i in range(1, NTILE):
        slab = slab + owned[i]
    slab_cells = pl.ds(pl.multiple_of(snd * SLAB, SLAB), SLAB)
    grad_ref[:, slab_cells] = slab
    size = jnp.abs(slab)
    top = size[:, 0:128]
    for c in range(1, CHUNKS):
        top = jnp.maximum(top, size[:, c * 128 : (c + 1) * 128])
    peaks[tile] = top

    mp, fin, mc = [], [], []
    for i, to, frm in plane:
        copy = pltpu.make_async_remote_copy(
            peaks.at[tile], peaks.at[tile], mp_send.at[i], mp_recv.at[i], (snd, to), MESH
        )
        copy.start()
        mp.append(copy)
    for i, to, frm in column:
        copy = pltpu.make_async_remote_copy(
            grad_ref.at[:, slab_cells],
            grad_ref.at[:, slab_cells],
            fin_send.at[i],
            fin_recv.at[i],
            (to, tile),
            MESH,
        )
        copy.start()
        fin.append(copy)
    for copy in mp:
        copy.wait()
    top = peaks[0]
    for i in range(1, NTILE):
        top = jnp.maximum(top, peaks[i])
    peaks2[snd] = top
    for i, to, frm in column:
        copy = pltpu.make_async_remote_copy(
            peaks2.at[snd], peaks2.at[snd], mc_send.at[i], mc_recv.at[i], (to, tile), MESH
        )
        copy.start()
        mc.append(copy)
    for copy in mc:
        copy.wait()
    top = peaks2[0]
    for i in range(1, NSND):
        top = jnp.maximum(top, peaks2[i])
    peak_ref[...] = top
    for copy in fin:
        copy.wait()


def finish(grad, peak, level_set, grad_out, next_out):
    scale = step_size / (jnp.max(peak[...]) + 1e-6)
    grad_out[:, 0:TOP] = grad[...]
    next_out[:, 0:TOP] = level_set[:, 0:TOP] - scale * grad[...]
    rest = level_set.shape[1] - TOP
    grad_out[:, TOP:] = jnp.zeros((TDEV, rest), jnp.float32)
    next_out[:, TOP:] = level_set[:, TOP:]


def shards(level_set, tile_home, footprints, adjoint_source, primal_fields):
    f32 = jnp.float32
    smem = pl.BlockSpec(memory_space=pltpu.SMEM)
    anywhere = pl.BlockSpec(memory_space=pl.ANY)
    vmem = pl.BlockSpec(memory_space=pltpu.VMEM)
    field = pltpu.VMEM((32, DEPTH, 128), f32)
    padded = pltpu.VMEM((34, DEPTH + 16, 128), f32)
    dma = pltpu.SemaphoreType.DMA
    grad, peak = pl.pallas_call(
        kernel,
        out_shape=(
            jax.ShapeDtypeStruct((TDEV, TOP), f32),
            jax.ShapeDtypeStruct((8, 128), f32),
        ),
        in_specs=[smem, smem, anywhere, anywhere, anywhere],
        out_specs=(vmem, vmem),
        scratch_shapes=[
            pltpu.VMEM(adjoint_source.shape, jnp.bfloat16),
            pltpu.VMEM(primal_fields.shape, jnp.bfloat16),
            pltpu.VMEM((NTILE, TDEV, SLAB), f32),
            pltpu.VMEM((NSND * ENTRIES, TILES), f32),
            pltpu.VMEM((NSND, SROWS, 128), f32),
            pltpu.VMEM((NSND * SROWS, 128), f32),
            field,
            field,
            field,
            field,
            field,
            field,
            padded,
            padded,
            field,
            pltpu.VMEM((NSND * SROWS, 128), f32),
            pltpu.VMEM((NSND, SROWS, 128), f32),
            pltpu.VMEM((NTILE, TDEV, SLAB), f32),
            pltpu.VMEM((NTILE, TDEV, SLAB), f32),
            pltpu.VMEM((NTILE, 8, 128), f32),
            pltpu.VMEM((NSND, 8, 128), f32),
            dma((3,)),
            dma((16,)),
            dma((16,)),
            dma((8,)),
            dma((8,)),
            dma((8,)),
            dma((8,)),
            dma((8,)),
            dma((8,)),
            dma((16,)),
            dma((16,)),
            dma((8,)),
            dma((8,)),
            dma((16,)),
            dma((16,)),
            dma((8,)),
            dma((8,)),
        ],
        compiler_params=pltpu.CompilerParams(
            collective_id=0, has_side_effects=True, vmem_limit_bytes=40 * 1024 * 1024
        ),
    )(footprints, tile_home, level_set, adjoint_source, primal_fields)
    out = jax.ShapeDtypeStruct(level_set.shape, f32)
    return pl.pallas_call(
        finish,
        out_shape=(out, out),
        in_specs=[vmem, vmem, vmem],
        out_specs=(vmem, vmem),
        compiler_params=pltpu.CompilerParams(vmem_limit_bytes=40 * 1024 * 1024),
    )(grad, peak, level_set)


def solution(mesh):
    return jax.shard_map(
        shards,
        mesh=mesh,
        in_specs=(
            P("tile", None),
            P(),
            P(("snd", "tile"), None),
            P(("snd", "tile"), None, None),
            P(("snd", "tile"), None, None, None),
        ),
        out_specs=(P("tile", None), P("tile", None)),
        check_vma=False,
    )
```

```python
import functools

import jax
import jax.numpy as jnp
from jax import lax
from jax.experimental import pallas as pl
from jax.experimental.pallas import tpu as pltpu
from jax.sharding import PartitionSpec as P

MESH = pl.DeviceIdType.MESH

TX = 16
DEPTH = 48
FOOT = 4
JACOBI = 8
NTILE = 16
NSND = 8
TDEV = 8
TILES = NTILE * TDEV
ENTRIES = FOOT * FOOT
TOP = DEPTH * TX * TX
SLAB = TOP // NSND
CHUNKS = SLAB // 128
SROWS = CHUNKS * ENTRIES
PIECES = 3
PCHUNKS = CHUNKS // PIECES
PCELLS = SLAB // PIECES
PROWS = SROWS // PIECES

VMEM_LIMIT = 60 * 1024 * 1024

log_low = -1.2
log_span = 2.5
front_width = 0.5
step_size = 0.5


def exchange_groups(blocks, lane):
    turned = [pltpu.roll(v, TX * g, 1) if g else v for g, v in enumerate(blocks)]
    for bit in range(3):
        step = 1 << bit
        upper = (lane & (TX * step)) != 0
        turned = [jnp.where(upper, turned[(i + step) % 8], turned[i]) for i in range(8)]
    return [pltpu.roll(turned[(8 - q) % 8], 128 - TX * q, 1) if q else turned[0] for q in range(8)]


def split3(x):
    hi = x.astype(jnp.bfloat16)
    rest = x - hi.astype(jnp.float32)
    mid = rest.astype(jnp.bfloat16)
    lo = (rest - mid.astype(jnp.float32)).astype(jnp.bfloat16)
    return hi, mid, lo


def onehot_dot(onehot, x):
    return sum(jnp.dot(onehot, part, preferred_element_type=jnp.float32) for part in split3(x))


def kernel(
    footprints,
    tile_home,
    level_set,
    adjoint_source,
    primal_fields,
    grad_ref,
    peak_ref,
    src_in,
    prim_in,
    gathered,
    request,
    picked,
    returned,
    source,
    diff21,
    diff10,
    conduct,
    inverse,
    slope,
    va,
    vb,
    adjoint_two,
    outgoing,
    arrived,
    partial,
    owned,
    peaks,
    peaks2,
    local_sem,
    ag_send,
    ag_recv,
    rq_send,
    rq_recv,
    pk_send,
    pk_recv,
    og_send,
    og_recv,
    rs_send,
    rs_recv,
    fin_send,
    fin_recv,
    mp_send,
    mp_recv,
    mc_send,
    mc_recv,
):
    snd = lax.axis_index("snd")
    tile = lax.axis_index("tile")
    x, y = tile // 4, tile % 4
    z, core = snd // 2, snd % 2

    plane = []
    for i in range(1, 16):
        dx, dy = i // 4, i % 4
        plane.append((i, ((x + dx) % 4) * 4 + (y + dy) % 4))
    column = []
    for i in range(1, 8):
        dz, dc = i // 2, i % 2
        column.append((i, ((z + dz) % 4) * 2 + (core + dc) % 2))

    barrier = pltpu.get_barrier_semaphore()
    for _, to in plane:
        pl.semaphore_signal(barrier, inc=1, device_id=(snd, to), device_id_type=MESH)
    for _, to in column:
        pl.semaphore_signal(barrier, inc=1, device_id=(to, tile), device_id_type=MESH)

    own = []
    for p in range(PIECES):
        start = pl.multiple_of(snd * SLAB + p * PCELLS, PCELLS)
        own.append(
            pltpu.make_async_copy(
                level_set.at[:, pl.ds(start, PCELLS)], gathered.at[p, tile], local_sem.at[p]
            )
        )
        own[-1].start()
    load_src = pltpu.make_async_copy(adjoint_source, src_in, local_sem.at[PIECES])
    load_prim = pltpu.make_async_copy(primal_fields, prim_in, local_sem.at[PIECES + 1])
    load_src.start()
    load_prim.start()

    sends = []

    def start(src, dst, send_sem, recv_sem, to):
        copy = pltpu.make_async_remote_copy(src, dst, send_sem, recv_sem, to, MESH)
        copy.start()
        sends.append(copy)
        return copy

    wanted_rows = lax.broadcasted_iota(jnp.int32, (ENTRIES, TILES), 0)
    stored_rows = lax.broadcasted_iota(jnp.int32, (ENTRIES, TILES), 1)
    wanted = jnp.zeros((ENTRIES, TILES), jnp.int32)
    for j in range(ENTRIES):
        wanted = jnp.where(wanted_rows == j, tile_home[footprints[0, j]], wanted)
    mine = pl.ds(pl.multiple_of(snd * ENTRIES, ENTRIES), ENTRIES)
    request[mine, :] = jnp.where(wanted == stored_rows, 1.0, 0.0)

    for copy in own:
        copy.wait()
    pl.semaphore_wait(barrier, 22)

    ag, rq = [], []
    for p in range(PIECES):
        block = gathered.at[p, tile]
        ag.append([start(block, block, ag_send.at[p, i], ag_recv.at[p, i], (snd, to)) for i, to in plane])
        if p == 0:
            for i, to in column:
                rows = request.at[mine]
                rq.append(start(rows, rows, rq_send.at[i], rq_recv.at[i], (to, tile)))

    lane = lax.broadcasted_iota(jnp.int32, (DEPTH, 128), 1)
    left = lane < 64

    def halves(top, bottom):
        return (
            jnp.where(left, top, pltpu.roll(bottom, 64, 1)),
            jnp.where(left, pltpu.roll(top, 64, 1), bottom),
        )

    load_src.wait()
    load_prim.wait()

    def lay_out(rp, carry):
        low = pl.ds(pl.multiple_of(rp * 128, 128), 128)
        high = pl.ds(pl.multiple_of(rp * 128 + 2048, 128), 128)
        even, odd = halves(
            src_in[0, :, low].astype(jnp.float32), src_in[0, :, high].astype(jnp.float32)
        )
        source[2 * rp] = even
        source[2 * rp + 1] = odd
        fields = [
            [prim_in[0, k, :, part].astype(jnp.float32) for part in (low, high)] for k in range(3)
        ]
        even, odd = halves(fields[2][0] - fields[1][0], fields[2][1] - fields[1][1])
        diff21[2 * rp] = even
        diff21[2 * rp + 1] = odd
        even, odd = halves(fields[1][0] - fields[0][0], fields[1][1] - fields[0][1])
        diff10[2 * rp] = even
        diff10[2 * rp + 1] = odd
        return carry

    lax.fori_loop(0, 16, lay_out, 0, unroll=4)

    zeros8 = jnp.zeros((34, 8, 128), jnp.float32)
    for buf in (va, vb):
        buf[:, 0:8, :] = zeros8
        buf[:, 56:64, :] = zeros8

    lane_in = lax.broadcasted_iota(jnp.int32, (128, 128), 0)
    lane_out = lax.broadcasted_iota(jnp.int32, (128, 128), 1)
    apart = lane_in - lane_out
    beside = ((apart == 1) | (apart == -1)) & (lane_in // 64 == lane_out // 64)
    beside = jnp.where(beside, 1.0, 0.0).astype(jnp.bfloat16)
    beside = jnp.concatenate([beside, beside], axis=0)

    for copy in rq:
        copy.wait_recv()
    onehot = request[...]
    pick = onehot.astype(jnp.bfloat16)
    place = onehot.T.astype(jnp.bfloat16)
    pk = []
    for p in range(PIECES):
        for copy in ag[p]:
            copy.wait_recv()
        for c in range(PCHUNKS):
            cells = gathered[p, :, :, c * 128 : (c + 1) * 128].reshape(TILES, 128)
            picked[p, :, c * ENTRIES : (c + 1) * ENTRIES, :] = onehot_dot(pick, cells).reshape(
                NSND, ENTRIES, 128
            )
        rows = pl.ds(pl.multiple_of(snd * SROWS + p * PROWS, PROWS), PROWS)
        for i, to in column:
            pk.append(
                start(picked.at[p, to], returned.at[rows], pk_send.at[p, i], pk_recv.at[p, i], (to, tile))
            )
        returned[rows, :] = picked[p, snd]
    for copy in pk:
        copy.wait_recv()

    lane8 = lax.broadcasted_iota(jnp.int32, (8, 128), 1)

    def block_rows(step, g):
        db, rest = step // 4, step % 4
        th, b1 = rest // 2, rest % 2
        entry = (2 * (g // 4) + b1) * 4 + g % 4
        first = (db * 16 + th) * ENTRIES + entry
        return pl.ds(first, 8, stride=2 * ENTRIES), pl.multiple_of(db * 8, 8), b1 * 16 + th * 8

    def enter(step, carry):
        blocks = []
        for g in range(8):
            rows, depth, row = block_rows(step, g)
            blocks.append(returned[rows, :])
        for q, phi in enumerate(exchange_groups(blocks, lane8)):
            smooth = jnp.tanh(phi / front_width)
            cond = jnp.exp(log_low + 0.5 * log_span * (1.0 + smooth))
            at = pl.ds(depth, 8)
            inv = 1.0 / (6.0 + cond)
            conduct[row + q, at, :] = cond
            inverse[row + q, at, :] = inv
            slope[row + q, at, :] = (
                cond * (0.5 * log_span / front_width) * (1.0 - smooth * smooth)
            )
            va[row + q + 1, pl.ds(depth + 8, 8), :] = source[row + q, at, :] * inv
        return carry

    lax.fori_loop(0, 24, enter, 0, unroll=8)

    def sweep(now, keep):
        now[0, 8:56, :] = jnp.where(left, 0.0, pltpu.roll(now[32, 8:56, :], 64, 1))
        now[33, 8:56, :] = jnp.where(left, pltpu.roll(now[1, 8:56, :], 64, 1), 0.0)
        v = now[1:33, 8:56, :].reshape(32 * DEPTH, 128)
        hi = v.astype(jnp.bfloat16)
        lo = (v - hi.astype(jnp.float32)).astype(jnp.bfloat16)
        columns = jnp.dot(
            jnp.concatenate([hi, lo], axis=1), beside, preferred_element_type=jnp.float32
        ).reshape(32, DEPTH, 128)
        for row in range(32):
            total = now[row + 1, 7:55, :] + now[row + 1, 9:57, :]
            total = total + (now[row, 8:56, :] + now[row + 2, 8:56, :])
            total = total + columns[row]
            keep(row, (source[row] + total) * inverse[row])

    def solve(now, later, last):
        def into(buf):
            def keep(row, value):
                buf[row + 1, 8:56, :] = value

            return keep

        def pair(_, carry):
            sweep(now, into(later))
            sweep(later, into(now))
            return carry

        lax.fori_loop(0, (JACOBI - 2) // 2, pair, 0)
        sweep(now, last)

    def between(row, value):
        adjoint_two[row] = value
        rhs = conduct[row] * value
        source[row] = rhs
        vb[row + 1, 8:56, :] = rhs * inverse[row]

    def gradient(row, value):
        va[row + 1, 8:56, :] = -slope[row] * (
            adjoint_two[row] * diff21[row] + value * diff10[row]
        )

    solve(va, vb, between)
    solve(vb, va, gradient)

    def leave(step, carry):
        _, depth, row = block_rows(step, 0)
        blocks = [va[row + q + 1, pl.ds(depth + 8, 8), :] for q in range(8)]
        for g, block in enumerate(exchange_groups(blocks, lane8)):
            rows, _, _ = block_rows(step, g)
            outgoing[rows, :] = block
        return carry

    lax.fori_loop(0, 24, leave, 0, unroll=8)

    og = []
    for p in range(PIECES):
        og.append([])
        for i, to in column:
            rows = pl.ds(pl.multiple_of(to * SROWS + p * PROWS, PROWS), PROWS)
            og[p].append(
                start(outgoing.at[rows], arrived.at[p, snd], og_send.at[p, i], og_recv.at[p, i], (to, tile))
            )
        rows = pl.ds(pl.multiple_of(snd * SROWS + p * PROWS, PROWS), PROWS)
        arrived[p, snd] = outgoing[rows, :]

    rs = []
    for p in range(PIECES):
        for copy in og[p]:
            copy.wait_recv()
        for c in range(PCHUNKS):
            cells = arrived[p, :, c * ENTRIES : (c + 1) * ENTRIES, :].reshape(TILES, 128)
            partial[p, :, :, c * 128 : (c + 1) * 128] = onehot_dot(place, cells).reshape(
                NTILE, TDEV, 128
            )
        rs.append(
            [
                start(partial.at[p, to], owned.at[p, tile], rs_send.at[p, i], rs_recv.at[p, i], (snd, to))
                for i, to in plane
            ]
        )
        owned[p, tile] = partial[p, tile]

    fin = []
    top = jnp.zeros((TDEV, 128), jnp.float32)
    for p in range(PIECES):
        for copy in rs[p]:
            copy.wait_recv()
        slab = owned[p, 0]
        for i in range(1, NTILE):
            slab = slab + owned[p, i]
        cells = pl.ds(pl.multiple_of(snd * SLAB + p * PCELLS, PCELLS), PCELLS)
        grad_ref[:, cells] = slab
        size = jnp.abs(slab)
        for c in range(PCHUNKS):
            top = jnp.maximum(top, size[:, c * 128 : (c + 1) * 128])
        if p == PIECES - 1:
            peaks[tile] = top
            mp = [
                start(peaks.at[tile], peaks.at[tile], mp_send.at[i], mp_recv.at[i], (snd, to))
                for i, to in plane
            ]
        block = grad_ref.at[:, cells]
        for i, to in column:
            fin.append(start(block, block, fin_send.at[p, i], fin_recv.at[p, i], (to, tile)))

    for copy in mp:
        copy.wait_recv()
    top = peaks[0]
    for i in range(1, NTILE):
        top = jnp.maximum(top, peaks[i])
    peaks2[snd] = top
    mc = [
        start(peaks2.at[snd], peaks2.at[snd], mc_send.at[i], mc_recv.at[i], (to, tile))
        for i, to in column
    ]
    for copy in mc:
        copy.wait_recv()
    top = peaks2[0]
    for i in range(1, NSND):
        top = jnp.maximum(top, peaks2[i])
    peak_ref[...] = top
    for copy in fin:
        copy.wait_recv()
    for copy in sends:
        copy.wait_send()


def finish(grad, peak, level_set, grad_out, next_out, grad_in, peak_in, level_in, blank, sem):
    rest = level_set.shape[1] - TOP
    head, tail = pl.ds(0, TOP), pl.ds(TOP, rest)

    def copy(i, src, dst):
        c = pltpu.make_async_copy(src, dst, sem.at[i])
        c.start()
        return c

    reads = [
        copy(0, level_set.at[:, tail], level_in.at[:, tail]),
        copy(1, peak, peak_in),
        copy(2, grad, grad_in),
        copy(3, level_set.at[:, head], level_in.at[:, head]),
    ]
    blank[...] = jnp.zeros((TDEV, rest), jnp.float32)
    writes = [copy(4, blank, grad_out.at[:, tail])]
    reads[0].wait()
    writes.append(copy(5, level_in.at[:, tail], next_out.at[:, tail]))
    for c in reads[1:3]:
        c.wait()
    writes.append(copy(6, grad_in, grad_out.at[:, head]))
    scale = step_size / (jnp.max(peak_in[...]) + 1e-6)
    reads[3].wait()
    level_in[:, head] = level_in[:, head] - scale * grad_in[...]
    writes.append(copy(7, level_in.at[:, head], next_out.at[:, head]))
    for c in writes:
        c.wait()


def shards(level_set, tile_home, footprints, adjoint_source, primal_fields):
    f32 = jnp.float32
    smem = pl.BlockSpec(memory_space=pltpu.SMEM)
    anywhere = pl.BlockSpec(memory_space=pltpu.HBM)
    vmem = pl.BlockSpec(memory_space=pltpu.VMEM)
    field = pltpu.VMEM((32, DEPTH, 128), f32)
    padded = pltpu.VMEM((34, DEPTH + 16, 128), f32)
    dma = pltpu.SemaphoreType.DMA
    grad, peak = pl.pallas_call(
        kernel,
        out_shape=(
            jax.ShapeDtypeStruct((TDEV, TOP), f32),
            jax.ShapeDtypeStruct((8, 128), f32),
        ),
        in_specs=[smem, smem, anywhere, anywhere, anywhere],
        out_specs=(vmem, vmem),
        scratch_shapes=[
            pltpu.VMEM(adjoint_source.shape, jnp.bfloat16),
            pltpu.VMEM(primal_fields.shape, jnp.bfloat16),
            pltpu.VMEM((PIECES, NTILE, TDEV, PCELLS), f32),
            pltpu.VMEM((NSND * ENTRIES, TILES), f32),
            pltpu.VMEM((PIECES, NSND, PROWS, 128), f32),
            pltpu.VMEM((NSND * SROWS, 128), f32),
            field,
            field,
            field,
            field,
            field,
            field,
            padded,
            padded,
            field,
            pltpu.VMEM((NSND * SROWS, 128), f32),
            pltpu.VMEM((PIECES, NSND, PROWS, 128), f32),
            pltpu.VMEM((PIECES, NTILE, TDEV, PCELLS), f32),
            pltpu.VMEM((PIECES, NTILE, TDEV, PCELLS), f32),
            pltpu.VMEM((NTILE, 8, 128), f32),
            pltpu.VMEM((NSND, 8, 128), f32),
            dma((PIECES + 2,)),
            dma((PIECES, NTILE)),
            dma((PIECES, NTILE)),
            dma((NSND,)),
            dma((NSND,)),
            dma((PIECES, NSND)),
            dma((PIECES, NSND)),
            dma((PIECES, NSND)),
            dma((PIECES, NSND)),
            dma((PIECES, NTILE)),
            dma((PIECES, NTILE)),
            dma((PIECES, NSND)),
            dma((PIECES, NSND)),
            dma((NTILE,)),
            dma((NTILE,)),
            dma((NSND,)),
            dma((NSND,)),
        ],
        compiler_params=pltpu.CompilerParams(
            collective_id=0, has_side_effects=True, vmem_limit_bytes=VMEM_LIMIT
        ),
    )(footprints, tile_home, level_set, adjoint_source, primal_fields)
    out = jax.ShapeDtypeStruct(level_set.shape, f32)
    return pl.pallas_call(
        finish,
        out_shape=(out, out),
        in_specs=[anywhere, anywhere, anywhere],
        out_specs=(anywhere, anywhere),
        scratch_shapes=[
            pltpu.VMEM((TDEV, TOP), f32),
            pltpu.VMEM((8, 128), f32),
            pltpu.VMEM(level_set.shape, f32),
            pltpu.VMEM((TDEV, level_set.shape[1] - TOP), f32),
            dma((8,)),
        ],
        compiler_params=pltpu.CompilerParams(vmem_limit_bytes=VMEM_LIMIT),
    )(grad, peak, level_set)


def solution(mesh):
    return jax.shard_map(
        shards,
        mesh=mesh,
        in_specs=(
            P("tile", None),
            P(),
            P(("snd", "tile"), None),
            P(("snd", "tile"), None, None),
            P(("snd", "tile"), None, None, None),
        ),
        out_specs=(P("tile", None), P("tile", None)),
        check_vma=False,
    )
```

```python
import functools

import jax
import jax.numpy as jnp
from jax import lax
from jax.experimental import pallas as pl
from jax.experimental.pallas import tpu as pltpu
from jax.sharding import PartitionSpec as P

MESH = pl.DeviceIdType.MESH

TX = 16
DEPTH = 48
FOOT = 4
JACOBI = 8
NTILE = 16
NSND = 8
TDEV = 8
TILES = NTILE * TDEV
ENTRIES = FOOT * FOOT
TOP = DEPTH * TX * TX
SLAB = TOP // NSND
CHUNKS = SLAB // 128
SROWS = CHUNKS * ENTRIES
DEPTHS = (16, 16, 16)
PIECES = len(DEPTHS)
FIRST = [sum(DEPTHS[:p]) for p in range(PIECES)]
PCHUNKS = [d // 4 for d in DEPTHS]
MOST = max(PCHUNKS)

PLANE = ((2, 2), (1, 2), (3, 2), (2, 1), (2, 3), (1, 1), (3, 3), (1, 3), (3, 1), (0, 2), (2, 0), (0, 1), (0, 3), (1, 0), (3, 0))
COLUMN = ((2, 1), (2, 0), (1, 1), (3, 1), (1, 0), (3, 0), (0, 1))

VMEM_LIMIT = 60 * 1024 * 1024

log_low = -1.2
log_span = 2.5
front_width = 0.5
step_size = 0.5


def exchange_groups(blocks, lane):
    turned = [pltpu.roll(v, TX * g, 1) if g else v for g, v in enumerate(blocks)]
    for bit in range(3):
        step = 1 << bit
        upper = (lane & (TX * step)) != 0
        turned = [jnp.where(upper, turned[(i + step) % 8], turned[i]) for i in range(8)]
    return [pltpu.roll(turned[(8 - q) % 8], 128 - TX * q, 1) if q else turned[0] for q in range(8)]


def split3(x):
    hi = x.astype(jnp.bfloat16)
    rest = x - hi.astype(jnp.float32)
    mid = rest.astype(jnp.bfloat16)
    lo = (rest - mid.astype(jnp.float32)).astype(jnp.bfloat16)
    return hi, mid, lo


def onehot_dot(onehot, x):
    return sum(jnp.dot(onehot, part, preferred_element_type=jnp.float32) for part in split3(x))


def within(p):
    return pl.ds(0, PCHUNKS[p] * 128)


def piece_cells(p, k):
    size = PCHUNKS[p] * 128
    return pl.ds(pl.multiple_of(FIRST[p] * TX * TX + k * size, 128), size)


def piece_rows(p, k):
    size = PCHUNKS[p] * ENTRIES
    return pl.ds(pl.multiple_of(FIRST[p] * 2 * ENTRIES + k * size, ENTRIES), size)


def piece_steps(p):
    return FIRST[p] // 2, (FIRST[p] + DEPTHS[p]) // 2


def kernel(
    footprints,
    tile_home,
    level_set,
    adjoint_source,
    primal_fields,
    grad_out,
    peak_ref,
    src_in,
    prim_in,
    gathered,
    request,
    picked,
    returned,
    source,
    diff21,
    diff10,
    conduct,
    inverse,
    slope,
    va,
    vb,
    adjoint_two,
    outgoing,
    arrived,
    partial,
    owned,
    peaks,
    peaks2,
    grad_ref,
    local_sem,
    ag_send,
    ag_recv,
    rq_send,
    rq_recv,
    pk_send,
    pk_recv,
    og_send,
    og_recv,
    rs_send,
    rs_recv,
    fin_send,
    fin_recv,
    mp_send,
    mp_recv,
    mc_send,
    mc_recv,
):
    snd = lax.axis_index("snd")
    tile = lax.axis_index("tile")
    x, y = tile // 4, tile % 4
    z, core = snd // 2, snd % 2

    plane = []
    for dx, dy in PLANE:
        plane.append((4 * dx + dy, ((x + dx) % 4) * 4 + (y + dy) % 4))
    column = []
    for dz, dc in COLUMN:
        column.append((2 * dz + dc, ((z + dz) % 4) * 2 + (core + dc) % 2))

    barrier = pltpu.get_barrier_semaphore()
    for _, to in plane:
        pl.semaphore_signal(barrier, inc=1, device_id=(snd, to), device_id_type=MESH)
    for _, to in column:
        pl.semaphore_signal(barrier, inc=1, device_id=(to, tile), device_id_type=MESH)

    own = []
    for p in range(PIECES):
        cells = piece_cells(p, snd)
        own.append(
            pltpu.make_async_copy(
                level_set.at[:, cells], gathered.at[p, tile, :, within(p)], local_sem.at[p]
            )
        )
        own[-1].start()
    load_src = pltpu.make_async_copy(adjoint_source, src_in, local_sem.at[PIECES])
    load_prim = pltpu.make_async_copy(primal_fields, prim_in, local_sem.at[PIECES + 1])
    load_src.start()
    load_prim.start()

    sends = []

    def start(src, dst, send_sem, recv_sem, to):
        copy = pltpu.make_async_remote_copy(src, dst, send_sem, recv_sem, to, MESH)
        copy.start()
        sends.append(copy)
        return copy

    def drain(count):
        for copy in sends[: len(sends) - count]:
            copy.wait_send()
        del sends[: len(sends) - count]

    wanted_rows = lax.broadcasted_iota(jnp.int32, (ENTRIES, TILES), 0)
    stored_rows = lax.broadcasted_iota(jnp.int32, (ENTRIES, TILES), 1)
    wanted = jnp.zeros((ENTRIES, TILES), jnp.int32)
    for j in range(ENTRIES):
        wanted = jnp.where(wanted_rows == j, tile_home[footprints[0, j]], wanted)
    mine = pl.ds(pl.multiple_of(snd * ENTRIES, ENTRIES), ENTRIES)
    request[mine, :] = jnp.where(wanted == stored_rows, 1.0, 0.0)

    for copy in own:
        copy.wait()
    pl.semaphore_wait(barrier, 22)

    ag, rq = [], []
    for p in range(PIECES):
        block = gathered.at[p, tile, :, within(p)]
        ag.append([start(block, block, ag_send.at[p, i], ag_recv.at[p, i], (snd, to)) for i, to in plane])
        if p == 0:
            for i, to in column:
                rows = request.at[mine]
                rq.append(start(rows, rows, rq_send.at[i], rq_recv.at[i], (to, tile)))

    lane = lax.broadcasted_iota(jnp.int32, (DEPTH, 128), 1)
    left = lane < 64

    def halves(top, bottom):
        return (
            jnp.where(left, top, pltpu.roll(bottom, 64, 1)),
            jnp.where(left, pltpu.roll(top, 64, 1), bottom),
        )

    load_src.wait()
    load_prim.wait()

    def lay_out(rp, carry):
        low = pl.ds(pl.multiple_of(rp * 128, 128), 128)
        high = pl.ds(pl.multiple_of(rp * 128 + 2048, 128), 128)
        even, odd = halves(
            src_in[0, :, low].astype(jnp.float32), src_in[0, :, high].astype(jnp.float32)
        )
        source[2 * rp] = even
        source[2 * rp + 1] = odd
        fields = [
            [prim_in[0, k, :, part].astype(jnp.float32) for part in (low, high)] for k in range(3)
        ]
        even, odd = halves(fields[2][0] - fields[1][0], fields[2][1] - fields[1][1])
        diff21[2 * rp] = even
        diff21[2 * rp + 1] = odd
        even, odd = halves(fields[1][0] - fields[0][0], fields[1][1] - fields[0][1])
        diff10[2 * rp] = even
        diff10[2 * rp + 1] = odd
        return carry

    lax.fori_loop(0, 16, lay_out, 0, unroll=4)

    zeros8 = jnp.zeros((34, 8, 128), jnp.float32)
    for buf in (va, vb):
        buf[:, 0:8, :] = zeros8
        buf[:, 56:64, :] = zeros8

    lane_in = lax.broadcasted_iota(jnp.int32, (128, 128), 0)
    lane_out = lax.broadcasted_iota(jnp.int32, (128, 128), 1)
    apart = lane_in - lane_out
    beside = ((apart == 1) | (apart == -1)) & (lane_in // 64 == lane_out // 64)
    beside = jnp.where(beside, 1.0, 0.0).astype(jnp.bfloat16)
    beside = jnp.concatenate([beside, beside], axis=0)

    for copy in rq:
        copy.wait_recv()
    onehot = request[...]
    pick = onehot.astype(jnp.bfloat16)
    place = onehot.T.astype(jnp.bfloat16)
    pk = []
    for p in range(PIECES):
        for copy in ag[p]:
            copy.wait_recv()
        for c in range(PCHUNKS[p]):
            cells = gathered[p, :, :, c * 128 : (c + 1) * 128].reshape(TILES, 128)
            picked[p, :, c * ENTRIES : (c + 1) * ENTRIES, :] = onehot_dot(pick, cells).reshape(
                NSND, ENTRIES, 128
            )
        rows = piece_rows(p, snd)
        pk.append(
            [
                start(picked.at[p, to, 0 : PCHUNKS[p] * ENTRIES], returned.at[rows], pk_send.at[p, i], pk_recv.at[p, i], (to, tile))
                for i, to in column
            ]
        )
        returned[rows, :] = picked[p, snd, 0 : PCHUNKS[p] * ENTRIES]

    drain(PIECES * 7)

    lane8 = lax.broadcasted_iota(jnp.int32, (8, 128), 1)

    def block_rows(step, g):
        db, rest = step // 4, step % 4
        th, b1 = rest // 2, rest % 2
        entry = (2 * (g // 4) + b1) * 4 + g % 4
        first = (db * 16 + th) * ENTRIES + entry
        return pl.ds(first, 8, stride=2 * ENTRIES), pl.multiple_of(db * 8, 8), b1 * 16 + th * 8

    def enter(step, carry):
        blocks = []
        for g in range(8):
            rows, depth, row = block_rows(step, g)
            blocks.append(returned[rows, :])
        for q, phi in enumerate(exchange_groups(blocks, lane8)):
            smooth = jnp.tanh(phi / front_width)
            cond = jnp.exp(log_low + 0.5 * log_span * (1.0 + smooth))
            at = pl.ds(depth, 8)
            inv = 1.0 / (6.0 + cond)
            conduct[row + q, at, :] = cond
            inverse[row + q, at, :] = inv
            slope[row + q, at, :] = (
                cond * (0.5 * log_span / front_width) * (1.0 - smooth * smooth)
            )
            va[row + q + 1, pl.ds(depth + 8, 8), :] = source[row + q, at, :] * inv
        return carry

    for p in range(PIECES):
        for copy in pk[p]:
            copy.wait_recv()
        lax.fori_loop(*piece_steps(p), enter, 0, unroll=min(8, DEPTHS[p] // 2))

    def sweep(now, keep):
        now[0, 8:56, :] = jnp.where(left, 0.0, pltpu.roll(now[32, 8:56, :], 64, 1))
        now[33, 8:56, :] = jnp.where(left, pltpu.roll(now[1, 8:56, :], 64, 1), 0.0)
        v = now[1:33, 8:56, :].reshape(32 * DEPTH, 128)
        hi = v.astype(jnp.bfloat16)
        lo = (v - hi.astype(jnp.float32)).astype(jnp.bfloat16)
        columns = jnp.dot(
            jnp.concatenate([hi, lo], axis=1), beside, preferred_element_type=jnp.float32
        ).reshape(32, DEPTH, 128)
        for row in range(32):
            total = now[row + 1, 7:55, :] + now[row + 1, 9:57, :]
            total = total + (now[row, 8:56, :] + now[row + 2, 8:56, :])
            total = total + columns[row]
            keep(row, (source[row] + total) * inverse[row])

    def solve(now, later, last):
        def into(buf):
            def keep(row, value):
                buf[row + 1, 8:56, :] = value

            return keep

        def pair(_, carry):
            sweep(now, into(later))
            sweep(later, into(now))
            return carry

        lax.fori_loop(0, (JACOBI - 2) // 2, pair, 0)
        sweep(now, last)

    def between(row, value):
        adjoint_two[row] = value
        rhs = conduct[row] * value
        source[row] = rhs
        vb[row + 1, 8:56, :] = rhs * inverse[row]

    def gradient(row, value):
        va[row + 1, 8:56, :] = -slope[row] * (
            adjoint_two[row] * diff21[row] + value * diff10[row]
        )

    solve(va, vb, between)
    solve(vb, va, gradient)

    def leave(step, carry):
        _, depth, row = block_rows(step, 0)
        blocks = [va[row + q + 1, pl.ds(depth + 8, 8), :] for q in range(8)]
        for g, block in enumerate(exchange_groups(blocks, lane8)):
            rows, _, _ = block_rows(step, g)
            outgoing[rows, :] = block
        return carry

    og = []
    for p in range(PIECES):
        lax.fori_loop(*piece_steps(p), leave, 0, unroll=min(8, DEPTHS[p] // 2))
        og.append([])
        for i, to in column:
            rows = piece_rows(p, to)
            og[p].append(
                start(outgoing.at[rows], arrived.at[p, snd, 0 : PCHUNKS[p] * ENTRIES], og_send.at[p, i], og_recv.at[p, i], (to, tile))
            )
        rows = piece_rows(p, snd)
        arrived[p, snd, 0 : PCHUNKS[p] * ENTRIES] = outgoing[rows, :]

    drain(PIECES * 7)

    rs = []
    for p in range(PIECES):
        for copy in og[p]:
            copy.wait_recv()
        for c in range(PCHUNKS[p]):
            cells = arrived[p, :, c * ENTRIES : (c + 1) * ENTRIES, :].reshape(TILES, 128)
            partial[p, :, :, c * 128 : (c + 1) * 128] = onehot_dot(place, cells).reshape(
                NTILE, TDEV, 128
            )
        rs.append(
            [
                start(partial.at[p, to, :, within(p)], owned.at[p, tile, :, within(p)], rs_send.at[p, i], rs_recv.at[p, i], (snd, to))
                for i, to in plane
            ]
        )
        owned[p, tile, :, within(p)] = partial[p, tile, :, within(p)]

    drain(PIECES * 15)

    fin = []
    top = jnp.zeros((TDEV, 128), jnp.float32)
    for p in range(PIECES):
        for copy in rs[p]:
            copy.wait_recv()
        slab = owned[p, 0, :, within(p)]
        for i in range(1, NTILE):
            slab = slab + owned[p, i, :, within(p)]
        cells = piece_cells(p, snd)
        grad_ref[:, cells] = slab
        size = jnp.abs(slab)
        for c in range(PCHUNKS[p]):
            top = jnp.maximum(top, size[:, c * 128 : (c + 1) * 128])
        if p == PIECES - 1:
            peaks[tile] = top
            mp = [
                start(peaks.at[tile], peaks.at[tile], mp_send.at[i], mp_recv.at[i], (snd, to))
                for i, to in plane
            ]
        block = grad_ref.at[:, cells]
        for i, to in column:
            fin.append(start(block, block, fin_send.at[p, i], fin_recv.at[p, i], (to, tile)))

    drain(15 + 7)

    for copy in mp:
        copy.wait_recv()
    top = peaks[0]
    for i in range(1, NTILE):
        top = jnp.maximum(top, peaks[i])
    peaks2[snd] = top
    mc = [
        start(peaks2.at[snd], peaks2.at[snd], mc_send.at[i], mc_recv.at[i], (to, tile))
        for i, to in column
    ]
    drain(7)
    for copy in fin:
        copy.wait_recv()
    store = pltpu.make_async_copy(grad_ref, grad_out, local_sem.at[0])
    store.start()
    for copy in mc:
        copy.wait_recv()
    top = peaks2[0]
    for i in range(1, NSND):
        top = jnp.maximum(top, peaks2[i])
    peak_ref[...] = top
    drain(0)
    store.wait()


def finish(grad, peak, level_set, grad_out, next_out, grad_in, peak_in, level_in, blank, sem):
    rest = level_set.shape[1] - TOP
    head, tail = pl.ds(0, TOP), pl.ds(TOP, rest)

    def copy(i, src, dst):
        c = pltpu.make_async_copy(src, dst, sem.at[i])
        c.start()
        return c

    reads = [
        copy(0, level_set.at[:, tail], level_in.at[:, tail]),
        copy(1, peak, peak_in),
        copy(2, grad, grad_in),
        copy(3, level_set.at[:, head], level_in.at[:, head]),
    ]
    blank[...] = jnp.zeros((TDEV, rest), jnp.float32)
    writes = [copy(4, blank, grad_out.at[:, tail])]
    reads[0].wait()
    writes.append(copy(5, level_in.at[:, tail], next_out.at[:, tail]))
    for c in reads[1:3]:
        c.wait()
    writes.append(copy(6, grad_in, grad_out.at[:, head]))
    scale = step_size / (jnp.max(peak_in[...]) + 1e-6)
    reads[3].wait()
    level_in[:, head] = level_in[:, head] - scale * grad_in[...]
    writes.append(copy(7, level_in.at[:, head], next_out.at[:, head]))
    for c in writes:
        c.wait()


def shards(level_set, tile_home, footprints, adjoint_source, primal_fields):
    f32 = jnp.float32
    smem = pl.BlockSpec(memory_space=pltpu.SMEM)
    anywhere = pl.BlockSpec(memory_space=pltpu.HBM)
    vmem = pl.BlockSpec(memory_space=pltpu.VMEM)
    field = pltpu.VMEM((32, DEPTH, 128), f32)
    padded = pltpu.VMEM((34, DEPTH + 16, 128), f32)
    dma = pltpu.SemaphoreType.DMA
    grad, peak = pl.pallas_call(
        kernel,
        out_shape=(
            jax.ShapeDtypeStruct((TDEV, TOP), f32),
            jax.ShapeDtypeStruct((8, 128), f32),
        ),
        in_specs=[smem, smem, anywhere, anywhere, anywhere],
        out_specs=(anywhere, vmem),
        scratch_shapes=[
            pltpu.VMEM(adjoint_source.shape, jnp.bfloat16),
            pltpu.VMEM(primal_fields.shape, jnp.bfloat16),
            pltpu.VMEM((PIECES, NTILE, TDEV, MOST * 128), f32),
            pltpu.VMEM((NSND * ENTRIES, TILES), f32),
            pltpu.VMEM((PIECES, NSND, MOST * ENTRIES, 128), f32),
            pltpu.VMEM((NSND * SROWS, 128), f32),
            field,
            field,
            field,
            field,
            field,
            field,
            padded,
            padded,
            field,
            pltpu.VMEM((NSND * SROWS, 128), f32),
            pltpu.VMEM((PIECES, NSND, MOST * ENTRIES, 128), f32),
            pltpu.VMEM((PIECES, NTILE, TDEV, MOST * 128), f32),
            pltpu.VMEM((PIECES, NTILE, TDEV, MOST * 128), f32),
            pltpu.VMEM((NTILE, 8, 128), f32),
            pltpu.VMEM((NSND, 8, 128), f32),
            pltpu.VMEM((TDEV, TOP), f32),
            dma((PIECES + 2,)),
            dma((PIECES, NTILE)),
            dma((PIECES, NTILE)),
            dma((NSND,)),
            dma((NSND,)),
            dma((PIECES, NSND)),
            dma((PIECES, NSND)),
            dma((PIECES, NSND)),
            dma((PIECES, NSND)),
            dma((PIECES, NTILE)),
            dma((PIECES, NTILE)),
            dma((PIECES, NSND)),
            dma((PIECES, NSND)),
            dma((NTILE,)),
            dma((NTILE,)),
            dma((NSND,)),
            dma((NSND,)),
        ],
        compiler_params=pltpu.CompilerParams(
            collective_id=0, has_side_effects=True, vmem_limit_bytes=VMEM_LIMIT
        ),
    )(footprints, tile_home, level_set, adjoint_source, primal_fields)
    out = jax.ShapeDtypeStruct(level_set.shape, f32)
    return pl.pallas_call(
        finish,
        out_shape=(out, out),
        in_specs=[anywhere, anywhere, anywhere],
        out_specs=(anywhere, anywhere),
        scratch_shapes=[
            pltpu.VMEM((TDEV, TOP), f32),
            pltpu.VMEM((8, 128), f32),
            pltpu.VMEM(level_set.shape, f32),
            pltpu.VMEM((TDEV, level_set.shape[1] - TOP), f32),
            dma((8,)),
        ],
        compiler_params=pltpu.CompilerParams(vmem_limit_bytes=VMEM_LIMIT),
    )(grad, peak, level_set)


def solution(mesh):
    return jax.shard_map(
        shards,
        mesh=mesh,
        in_specs=(
            P("tile", None),
            P(),
            P(("snd", "tile"), None),
            P(("snd", "tile"), None, None),
            P(("snd", "tile"), None, None, None),
        ),
        out_specs=(P("tile", None), P("tile", None)),
        check_vma=False,
    )
```

```python
import functools

import jax
import jax.numpy as jnp
from jax import lax
from jax.experimental import pallas as pl
from jax.experimental.pallas import tpu as pltpu
from jax.sharding import PartitionSpec as P

MESH = pl.DeviceIdType.MESH

TX = 16
DEPTH = 48
FOOT = 4
JACOBI = 8
NTILE = 16
NSND = 8
TDEV = 8
TILES = NTILE * TDEV
ENTRIES = FOOT * FOOT
TOP = DEPTH * TX * TX
SLAB = TOP // NSND
CHUNKS = SLAB // 128
SROWS = CHUNKS * ENTRIES
DEPTHS = (8, 8, 8, 8, 8, 8)
PIECES = len(DEPTHS)
FIRST = [sum(DEPTHS[:p]) for p in range(PIECES)]
PCHUNKS = [d // 4 for d in DEPTHS]
MOST = max(PCHUNKS)

PLANE = ((2, 2), (1, 2), (3, 2), (2, 1), (2, 3), (1, 1), (3, 3), (1, 3), (3, 1), (0, 2), (2, 0), (0, 1), (0, 3), (1, 0), (3, 0))
COLUMN = ((2, 1), (2, 0), (1, 1), (3, 1), (1, 0), (3, 0), (0, 1))

VMEM_LIMIT = 60 * 1024 * 1024

log_low = -1.2
log_span = 2.5
front_width = 0.5
step_size = 0.5


def exchange_groups(blocks, lane):
    turned = [pltpu.roll(v, TX * g, 1) if g else v for g, v in enumerate(blocks)]
    for bit in range(3):
        step = 1 << bit
        upper = (lane & (TX * step)) != 0
        turned = [jnp.where(upper, turned[(i + step) % 8], turned[i]) for i in range(8)]
    return [pltpu.roll(turned[(8 - q) % 8], 128 - TX * q, 1) if q else turned[0] for q in range(8)]


def split3(x):
    hi = x.astype(jnp.bfloat16)
    rest = x - hi.astype(jnp.float32)
    mid = rest.astype(jnp.bfloat16)
    lo = (rest - mid.astype(jnp.float32)).astype(jnp.bfloat16)
    return hi, mid, lo


def onehot_dot(onehot, x):
    return sum(jnp.dot(onehot, part, preferred_element_type=jnp.float32) for part in split3(x))


def within(p):
    return pl.ds(0, PCHUNKS[p] * 128)


def piece_cells(p, k):
    size = PCHUNKS[p] * 128
    return pl.ds(pl.multiple_of(FIRST[p] * TX * TX + k * size, 128), size)


def piece_rows(p, k):
    size = PCHUNKS[p] * ENTRIES
    return pl.ds(pl.multiple_of(FIRST[p] * 2 * ENTRIES + k * size, ENTRIES), size)


def piece_seven(p):
    return pl.ds(0, 7 * PCHUNKS[p] * ENTRIES)


def piece_steps(p):
    return FIRST[p] // 2, (FIRST[p] + DEPTHS[p]) // 2


def kernel(
    footprints,
    tile_home,
    level_set,
    adjoint_source,
    primal_fields,
    grad_out,
    peak_ref,
    src_in,
    prim_in,
    gathered,
    request,
    picked,
    returned,
    source,
    diff21,
    diff10,
    conduct,
    inverse,
    slope,
    va,
    vb,
    adjoint_two,
    outgoing,
    arrived,
    partial,
    owned,
    peaks,
    peaks2,
    grad_ref,
    local_sem,
    ag_send,
    ag_recv,
    rq_send,
    rq_recv,
    pk_send,
    pk_recv,
    og_send,
    og_recv,
    rs_send,
    rs_recv,
    fin_send,
    fin_recv,
    mp_send,
    mp_recv,
    mc_send,
    mc_recv,
):
    snd = lax.axis_index("snd")
    tile = lax.axis_index("tile")
    x, y = tile // 4, tile % 4
    z, core = snd // 2, snd % 2

    plane = []
    for dx, dy in PLANE:
        plane.append((x + dx) % 4 * 4 + (y + dy) % 4)
    column = []
    for dz, dc in COLUMN:
        column.append((z + dz) % 4 * 2 + (core + dc) % 2)

    barrier = pltpu.get_barrier_semaphore()
    for to in plane:
        pl.semaphore_signal(barrier, inc=1, device_id=(snd, to), device_id_type=MESH)
    for to in column:
        pl.semaphore_signal(barrier, inc=1, device_id=(to, tile), device_id_type=MESH)

    own = []
    for p in range(PIECES):
        cells = piece_cells(p, snd)
        own.append(
            pltpu.make_async_copy(
                level_set.at[:, cells], gathered.at[p, tile, :, within(p)], local_sem.at[p]
            )
        )
        own[-1].start()
    load_src = pltpu.make_async_copy(adjoint_source, src_in, local_sem.at[PIECES])
    load_prim = pltpu.make_async_copy(primal_fields, prim_in, local_sem.at[PIECES + 1])
    load_src.start()
    load_prim.start()

    sends = []

    def send_all(parts, send_sem, recv_sem, whole):
        for src, dst, to in parts:
            pltpu.make_async_remote_copy(src, dst, send_sem, recv_sem, to, MESH).start()
        sends.append((whole, send_sem))
        return whole, recv_sem

    def wait_all(pair):
        whole, sem = pair
        pltpu.make_async_copy(whole, whole, sem).wait()

    waited = [0]

    def drain(mark):
        for pair in sends[waited[0] : mark]:
            wait_all(pair)
        waited[0] = mark

    wanted_rows = lax.broadcasted_iota(jnp.int32, (ENTRIES, TILES), 0)
    stored_rows = lax.broadcasted_iota(jnp.int32, (ENTRIES, TILES), 1)
    wanted = jnp.zeros((ENTRIES, TILES), jnp.int32)
    for j in range(ENTRIES):
        wanted = jnp.where(wanted_rows == j, tile_home[footprints[0, j]], wanted)
    mine = pl.ds(pl.multiple_of(snd * ENTRIES, ENTRIES), ENTRIES)
    request[mine, :] = jnp.where(wanted == stored_rows, 1.0, 0.0)

    for copy in own:
        copy.wait()
    pl.semaphore_wait(barrier, 22)

    ag = []
    for p in range(PIECES):
        block = gathered.at[p, tile, :, within(p)]
        ag.append(
            send_all(
                [(block, block, (snd, to)) for to in plane],
                ag_send.at[p],
                ag_recv.at[p],
                gathered.at[p, 0:15, :, within(p)],
            )
        )
        if p == 0:
            rows = request.at[mine]
            rq = send_all(
                [(rows, rows, (to, tile)) for to in column],
                rq_send.at[0],
                rq_recv.at[0],
                request.at[0 : 7 * ENTRIES],
            )

    lane = lax.broadcasted_iota(jnp.int32, (DEPTH, 128), 1)
    left = lane < 64

    def halves(top, bottom):
        return (
            jnp.where(left, top, pltpu.roll(bottom, 64, 1)),
            jnp.where(left, pltpu.roll(top, 64, 1), bottom),
        )

    load_src.wait()
    load_prim.wait()

    def lay_out(rp, carry):
        low = pl.ds(pl.multiple_of(rp * 128, 128), 128)
        high = pl.ds(pl.multiple_of(rp * 128 + 2048, 128), 128)
        even, odd = halves(
            src_in[0, :, low].astype(jnp.float32), src_in[0, :, high].astype(jnp.float32)
        )
        source[2 * rp] = even
        source[2 * rp + 1] = odd
        fields = [
            [prim_in[0, k, :, part].astype(jnp.float32) for part in (low, high)] for k in range(3)
        ]
        even, odd = halves(fields[2][0] - fields[1][0], fields[2][1] - fields[1][1])
        diff21[2 * rp] = even
        diff21[2 * rp + 1] = odd
        even, odd = halves(fields[1][0] - fields[0][0], fields[1][1] - fields[0][1])
        diff10[2 * rp] = even
        diff10[2 * rp + 1] = odd
        return carry

    lax.fori_loop(0, 16, lay_out, 0, unroll=4)

    zeros8 = jnp.zeros((34, 8, 128), jnp.float32)
    for buf in (va, vb):
        buf[:, 0:8, :] = zeros8
        buf[:, 56:64, :] = zeros8

    lane_in = lax.broadcasted_iota(jnp.int32, (128, 128), 0)
    lane_out = lax.broadcasted_iota(jnp.int32, (128, 128), 1)
    apart = lane_in - lane_out
    beside = ((apart == 1) | (apart == -1)) & (lane_in // 64 == lane_out // 64)
    beside = jnp.where(beside, 1.0, 0.0).astype(jnp.bfloat16)
    beside = jnp.concatenate([beside, beside], axis=0)

    wait_all(rq)
    onehot = request[...]
    pick = onehot.astype(jnp.bfloat16)
    place = onehot.T.astype(jnp.bfloat16)
    gather_sends = len(sends)
    pk = []
    for p in range(PIECES):
        wait_all(ag[p])
        for c in range(PCHUNKS[p]):
            cells = gathered[p, :, :, c * 128 : (c + 1) * 128].reshape(TILES, 128)
            picked[p, :, c * ENTRIES : (c + 1) * ENTRIES, :] = onehot_dot(pick, cells).reshape(
                NSND, ENTRIES, 128
            )
        rows = piece_rows(p, snd)
        size = PCHUNKS[p] * ENTRIES
        pk.append(
            send_all(
                [(picked.at[p, to, 0:size], returned.at[rows], (to, tile)) for to in column],
                pk_send.at[p],
                pk_recv.at[p],
                returned.at[piece_seven(p)],
            )
        )
        returned[rows, :] = picked[p, snd, 0 : PCHUNKS[p] * ENTRIES]

    drain(gather_sends)

    lane8 = lax.broadcasted_iota(jnp.int32, (8, 128), 1)

    def block_rows(step, g):
        db, rest = step // 4, step % 4
        th, b1 = rest // 2, rest % 2
        entry = (2 * (g // 4) + b1) * 4 + g % 4
        first = (db * 16 + th) * ENTRIES + entry
        return pl.ds(first, 8, stride=2 * ENTRIES), pl.multiple_of(db * 8, 8), b1 * 16 + th * 8

    def enter(step, carry):
        blocks = []
        for g in range(8):
            rows, depth, row = block_rows(step, g)
            blocks.append(returned[rows, :])
        for q, phi in enumerate(exchange_groups(blocks, lane8)):
            smooth = jnp.tanh(phi / front_width)
            cond = jnp.exp(log_low + 0.5 * log_span * (1.0 + smooth))
            at = pl.ds(depth, 8)
            inv = 1.0 / (6.0 + cond)
            conduct[row + q, at, :] = cond
            inverse[row + q, at, :] = inv
            slope[row + q, at, :] = (
                cond * (0.5 * log_span / front_width) * (1.0 - smooth * smooth)
            )
            va[row + q + 1, pl.ds(depth + 8, 8), :] = source[row + q, at, :] * inv
        return carry

    for p in range(PIECES):
        wait_all(pk[p])
        lax.fori_loop(*piece_steps(p), enter, 0, unroll=min(8, DEPTHS[p] // 2))

    def sweep(now, keep):
        now[0, 8:56, :] = jnp.where(left, 0.0, pltpu.roll(now[32, 8:56, :], 64, 1))
        now[33, 8:56, :] = jnp.where(left, pltpu.roll(now[1, 8:56, :], 64, 1), 0.0)
        v = now[1:33, 8:56, :].reshape(32 * DEPTH, 128)
        hi = v.astype(jnp.bfloat16)
        lo = (v - hi.astype(jnp.float32)).astype(jnp.bfloat16)
        columns = jnp.dot(
            jnp.concatenate([hi, lo], axis=1), beside, preferred_element_type=jnp.float32
        ).reshape(32, DEPTH, 128)
        for row in range(32):
            total = now[row + 1, 7:55, :] + now[row + 1, 9:57, :]
            total = total + (now[row, 8:56, :] + now[row + 2, 8:56, :])
            total = total + columns[row]
            keep(row, (source[row] + total) * inverse[row])

    def solve(now, later, last):
        def into(buf):
            def keep(row, value):
                buf[row + 1, 8:56, :] = value

            return keep

        def pair(_, carry):
            sweep(now, into(later))
            sweep(later, into(now))
            return carry

        lax.fori_loop(0, (JACOBI - 2) // 2, pair, 0)
        sweep(now, last)

    def between(row, value):
        adjoint_two[row] = value
        rhs = conduct[row] * value
        source[row] = rhs
        vb[row + 1, 8:56, :] = rhs * inverse[row]

    def gradient(row, value):
        va[row + 1, 8:56, :] = -slope[row] * (
            adjoint_two[row] * diff21[row] + value * diff10[row]
        )

    solve(va, vb, between)
    solve(vb, va, gradient)

    def leave(step, carry):
        _, depth, row = block_rows(step, 0)
        blocks = [va[row + q + 1, pl.ds(depth + 8, 8), :] for q in range(8)]
        for g, block in enumerate(exchange_groups(blocks, lane8)):
            rows, _, _ = block_rows(step, g)
            outgoing[rows, :] = block
        return carry

    pick_sends = len(sends)
    og = []
    for p in range(PIECES):
        lax.fori_loop(*piece_steps(p), leave, 0, unroll=min(8, DEPTHS[p] // 2))
        size = PCHUNKS[p] * ENTRIES
        og.append(
            send_all(
                [
                    (outgoing.at[piece_rows(p, to)], arrived.at[p, snd, 0:size], (to, tile))
                    for to in column
                ],
                og_send.at[p],
                og_recv.at[p],
                arrived.at[p, 0:7, 0:size],
            )
        )
        rows = piece_rows(p, snd)
        arrived[p, snd, 0 : PCHUNKS[p] * ENTRIES] = outgoing[rows, :]

    drain(pick_sends)

    og_sends = len(sends)
    rs = []
    for p in range(PIECES):
        wait_all(og[p])
        for c in range(PCHUNKS[p]):
            cells = arrived[p, :, c * ENTRIES : (c + 1) * ENTRIES, :].reshape(TILES, 128)
            partial[p, :, :, c * 128 : (c + 1) * 128] = onehot_dot(place, cells).reshape(
                NTILE, TDEV, 128
            )
        rs.append(
            send_all(
                [
                    (partial.at[p, to, :, within(p)], owned.at[p, tile, :, within(p)], (snd, to))
                    for to in plane
                ],
                rs_send.at[p],
                rs_recv.at[p],
                owned.at[p, 0:15, :, within(p)],
            )
        )
        owned[p, tile, :, within(p)] = partial[p, tile, :, within(p)]

    drain(og_sends)

    rs_sends = len(sends)
    fin = []
    top = jnp.zeros((TDEV, 128), jnp.float32)
    for p in range(PIECES):
        wait_all(rs[p])
        slab = owned[p, 0, :, within(p)]
        for i in range(1, NTILE):
            slab = slab + owned[p, i, :, within(p)]
        cells = piece_cells(p, snd)
        grad_ref[:, cells] = slab
        size = jnp.abs(slab)
        for c in range(PCHUNKS[p]):
            top = jnp.maximum(top, size[:, c * 128 : (c + 1) * 128])
        if p == PIECES - 1:
            peaks[tile] = jnp.max(top, axis=0, keepdims=True)
            peak = peaks.at[tile]
            mp = send_all(
                [(peak, peak, (snd, to)) for to in plane],
                mp_send.at[0],
                mp_recv.at[0],
                peaks.at[0:15],
            )
        block = grad_ref.at[:, cells]
        fin.append(
            send_all(
                [(block, block, (to, tile)) for to in column],
                fin_send.at[p],
                fin_recv.at[p],
                grad_ref.at[:, pl.ds(0, 7 * PCHUNKS[p] * 128)],
            )
        )

    drain(rs_sends)

    wait_all(mp)
    peaks2[snd] = jnp.max(peaks[...], axis=0)
    peak = peaks2.at[snd]
    mc = send_all(
        [(peak, peak, (to, tile)) for to in column], mc_send.at[0], mc_recv.at[0], peaks2.at[0:7]
    )
    drain(len(sends) - 1)
    for pair in fin:
        wait_all(pair)
    store = pltpu.make_async_copy(grad_ref, grad_out, local_sem.at[0])
    store.start()
    wait_all(mc)
    peak_ref[...] = jnp.broadcast_to(jnp.max(peaks2[...], axis=0), (8, 128))
    drain(len(sends))
    store.wait()


def finish(grad, peak, level_set, grad_out, next_out, grad_in, peak_in, level_in, blank, sem):
    rest = level_set.shape[1] - TOP
    head, tail = pl.ds(0, TOP), pl.ds(TOP, rest)

    def copy(i, src, dst):
        c = pltpu.make_async_copy(src, dst, sem.at[i])
        c.start()
        return c

    reads = [
        copy(0, level_set.at[:, tail], level_in.at[:, tail]),
        copy(1, peak, peak_in),
        copy(2, grad, grad_in),
        copy(3, level_set.at[:, head], level_in.at[:, head]),
    ]
    blank[...] = jnp.zeros((TDEV, rest), jnp.float32)
    writes = [copy(4, blank, grad_out.at[:, tail])]
    reads[0].wait()
    writes.append(copy(5, level_in.at[:, tail], next_out.at[:, tail]))
    for c in reads[1:3]:
        c.wait()
    writes.append(copy(6, grad_in, grad_out.at[:, head]))
    scale = step_size / (jnp.max(peak_in[...]) + 1e-6)
    reads[3].wait()
    level_in[:, head] = level_in[:, head] - scale * grad_in[...]
    writes.append(copy(7, level_in.at[:, head], next_out.at[:, head]))
    for c in writes:
        c.wait()


def shards(level_set, tile_home, footprints, adjoint_source, primal_fields):
    f32 = jnp.float32
    smem = pl.BlockSpec(memory_space=pltpu.SMEM)
    anywhere = pl.BlockSpec(memory_space=pltpu.HBM)
    vmem = pl.BlockSpec(memory_space=pltpu.VMEM)
    field = pltpu.VMEM((32, DEPTH, 128), f32)
    padded = pltpu.VMEM((34, DEPTH + 16, 128), f32)
    dma = pltpu.SemaphoreType.DMA
    grad, peak = pl.pallas_call(
        kernel,
        out_shape=(
            jax.ShapeDtypeStruct((TDEV, TOP), f32),
            jax.ShapeDtypeStruct((8, 128), f32),
        ),
        in_specs=[smem, smem, anywhere, anywhere, anywhere],
        out_specs=(anywhere, vmem),
        scratch_shapes=[
            pltpu.VMEM(adjoint_source.shape, jnp.bfloat16),
            pltpu.VMEM(primal_fields.shape, jnp.bfloat16),
            pltpu.VMEM((PIECES, NTILE, TDEV, MOST * 128), f32),
            pltpu.VMEM((NSND * ENTRIES, TILES), f32),
            pltpu.VMEM((PIECES, NSND, MOST * ENTRIES, 128), f32),
            pltpu.VMEM((NSND * SROWS, 128), f32),
            field,
            field,
            field,
            field,
            field,
            field,
            padded,
            padded,
            field,
            pltpu.VMEM((NSND * SROWS, 128), f32),
            pltpu.VMEM((PIECES, NSND, MOST * ENTRIES, 128), f32),
            pltpu.VMEM((PIECES, NTILE, TDEV, MOST * 128), f32),
            pltpu.VMEM((PIECES, NTILE, TDEV, MOST * 128), f32),
            pltpu.VMEM((NTILE, 1, 128), f32),
            pltpu.VMEM((NSND, 1, 128), f32),
            pltpu.VMEM((TDEV, TOP), f32),
            dma((PIECES + 2,)),
            dma((PIECES,)),
            dma((PIECES,)),
            dma((PIECES,)),
            dma((PIECES,)),
            dma((PIECES,)),
            dma((PIECES,)),
            dma((PIECES,)),
            dma((PIECES,)),
            dma((PIECES,)),
            dma((PIECES,)),
            dma((PIECES,)),
            dma((PIECES,)),
            dma((PIECES,)),
            dma((PIECES,)),
            dma((PIECES,)),
            dma((PIECES,)),
        ],
        compiler_params=pltpu.CompilerParams(
            collective_id=0, has_side_effects=True, vmem_limit_bytes=VMEM_LIMIT
        ),
    )(footprints, tile_home, level_set, adjoint_source, primal_fields)
    out = jax.ShapeDtypeStruct(level_set.shape, f32)
    return pl.pallas_call(
        finish,
        out_shape=(out, out),
        in_specs=[anywhere, anywhere, anywhere],
        out_specs=(anywhere, anywhere),
        scratch_shapes=[
            pltpu.VMEM((TDEV, TOP), f32),
            pltpu.VMEM((8, 128), f32),
            pltpu.VMEM(level_set.shape, f32),
            pltpu.VMEM((TDEV, level_set.shape[1] - TOP), f32),
            dma((8,)),
        ],
        compiler_params=pltpu.CompilerParams(vmem_limit_bytes=VMEM_LIMIT),
    )(grad, peak, level_set)


def solution(mesh):
    return jax.shard_map(
        shards,
        mesh=mesh,
        in_specs=(
            P("tile", None),
            P(),
            P(("snd", "tile"), None),
            P(("snd", "tile"), None, None),
            P(("snd", "tile"), None, None, None),
        ),
        out_specs=(P("tile", None), P("tile", None)),
        check_vma=False,
    )
```

```python
import functools

import jax
import jax.numpy as jnp
from jax import lax
from jax.experimental import pallas as pl
from jax.experimental.pallas import tpu as pltpu
from jax.sharding import PartitionSpec as P

MESH = pl.DeviceIdType.MESH

TX = 16
DEPTH = 48
FOOT = 4
JACOBI = 8
NTILE = 16
NSND = 8
TDEV = 8
TILES = NTILE * TDEV
ENTRIES = FOOT * FOOT
TOP = DEPTH * TX * TX
SLAB = TOP // NSND
CHUNKS = SLAB // 128
SROWS = CHUNKS * ENTRIES


class Pieces:
    def __init__(self, depths):
        self.depths = depths
        self.count = len(depths)
        self.first = [sum(depths[:p]) for p in range(self.count)]
        self.chunks = [d // 4 for d in depths]
        self.most = max(self.chunks)

    def within(self, p):
        return pl.ds(0, self.chunks[p] * 128)

    def cells(self, p, k):
        size = self.chunks[p] * 128
        return pl.ds(pl.multiple_of(self.first[p] * TX * TX + k * size, 128), size)

    def rows(self, p, k):
        size = self.chunks[p] * ENTRIES
        return pl.ds(pl.multiple_of(self.first[p] * 2 * ENTRIES + k * size, ENTRIES), size)

    def seven(self, p):
        return pl.ds(0, 7 * self.chunks[p] * ENTRIES)

    def steps(self, p):
        return self.first[p] // 2, (self.first[p] + self.depths[p]) // 2


FETCH = Pieces((8, 8, 8, 8, 8, 8))
GIVE = Pieces((8, 8, 8, 8, 8, 8))

PLANE = ((2, 2), (1, 2), (3, 2), (2, 1), (2, 3), (1, 1), (3, 3), (1, 3), (3, 1), (0, 2), (2, 0), (0, 1), (0, 3), (1, 0), (3, 0))
COLUMN = ((2, 1), (2, 0), (1, 1), (3, 1), (1, 0), (3, 0), (0, 1))

VMEM_LIMIT = 60 * 1024 * 1024

log_low = -1.2
log_span = 2.5
front_width = 0.5
step_size = 0.5


def exchange_groups(blocks, lane):
    turned = [pltpu.roll(v, TX * g, 1) if g else v for g, v in enumerate(blocks)]
    for bit in range(3):
        step = 1 << bit
        upper = (lane & (TX * step)) != 0
        turned = [jnp.where(upper, turned[(i + step) % 8], turned[i]) for i in range(8)]
    return [pltpu.roll(turned[(8 - q) % 8], 128 - TX * q, 1) if q else turned[0] for q in range(8)]


def split2(x):
    hi = x.astype(jnp.bfloat16)
    return hi, (x - hi.astype(jnp.float32)).astype(jnp.bfloat16)


def onehot_dot(onehot, x):
    return sum(jnp.dot(onehot, part, preferred_element_type=jnp.float32) for part in split2(x))


def kernel(
    footprints,
    tile_home,
    level_set,
    adjoint_source,
    primal_fields,
    grad_out,
    peak_ref,
    src_in,
    prim_in,
    gathered,
    request,
    picked,
    returned,
    source,
    diff21,
    diff10,
    conduct,
    inverse,
    slope,
    va,
    vb,
    adjoint_two,
    outgoing,
    arrived,
    partial,
    owned,
    peaks,
    peaks2,
    grad_ref,
    local_sem,
    ag_send,
    ag_recv,
    rq_send,
    rq_recv,
    pk_send,
    pk_recv,
    og_send,
    og_recv,
    rs_send,
    rs_recv,
    fin_send,
    fin_recv,
    mp_send,
    mp_recv,
    mc_send,
    mc_recv,
):
    snd = lax.axis_index("snd")
    tile = lax.axis_index("tile")
    x, y = tile // 4, tile % 4
    z, core = snd // 2, snd % 2

    plane = []
    for dx, dy in PLANE:
        plane.append((x + dx) % 4 * 4 + (y + dy) % 4)
    column = []
    for dz, dc in COLUMN:
        column.append((z + dz) % 4 * 2 + (core + dc) % 2)

    barrier = pltpu.get_barrier_semaphore()
    for to in plane:
        pl.semaphore_signal(barrier, inc=1, device_id=(snd, to), device_id_type=MESH)
    for to in column:
        pl.semaphore_signal(barrier, inc=1, device_id=(to, tile), device_id_type=MESH)

    own = []
    for p in range(FETCH.count):
        cells = FETCH.cells(p, snd)
        own.append(
            pltpu.make_async_copy(
                level_set.at[:, cells], gathered.at[p, tile, :, FETCH.within(p)], local_sem.at[p]
            )
        )
        own[-1].start()
    load_src = pltpu.make_async_copy(adjoint_source, src_in, local_sem.at[FETCH.count])
    load_prim = pltpu.make_async_copy(primal_fields, prim_in, local_sem.at[FETCH.count + 1])
    load_src.start()
    load_prim.start()

    sends = []

    def send_all(parts, send_sem, recv_sem, whole):
        for src, dst, to in parts:
            pltpu.make_async_remote_copy(src, dst, send_sem, recv_sem, to, MESH).start()
        sends.append((whole, send_sem))
        return whole, recv_sem

    def wait_all(pair):
        whole, sem = pair
        pltpu.make_async_copy(whole, whole, sem).wait()

    waited = [0]

    def drain(mark):
        for pair in sends[waited[0] : mark]:
            wait_all(pair)
        waited[0] = mark

    wanted_rows = lax.broadcasted_iota(jnp.int32, (ENTRIES, TILES), 0)
    stored_rows = lax.broadcasted_iota(jnp.int32, (ENTRIES, TILES), 1)
    wanted = jnp.zeros((ENTRIES, TILES), jnp.int32)
    for j in range(ENTRIES):
        wanted = jnp.where(wanted_rows == j, tile_home[footprints[0, j]], wanted)
    mine = pl.ds(pl.multiple_of(snd * ENTRIES, ENTRIES), ENTRIES)
    request[mine, :] = jnp.where(wanted == stored_rows, 1.0, 0.0)

    for copy in own:
        copy.wait()
    pl.semaphore_wait(barrier, 22)

    ag = []
    for p in range(FETCH.count):
        block = gathered.at[p, tile, :, FETCH.within(p)]
        ag.append(
            send_all(
                [(block, block, (snd, to)) for to in plane],
                ag_send.at[p],
                ag_recv.at[p],
                gathered.at[p, 0:15, :, FETCH.within(p)],
            )
        )
        if p == 0:
            rows = request.at[mine]
            rq = send_all(
                [(rows, rows, (to, tile)) for to in column],
                rq_send.at[0],
                rq_recv.at[0],
                request.at[0 : 7 * ENTRIES],
            )

    lane = lax.broadcasted_iota(jnp.int32, (DEPTH, 128), 1)
    left = lane < 64

    def halves(top, bottom):
        return (
            jnp.where(left, top, pltpu.roll(bottom, 64, 1)),
            jnp.where(left, pltpu.roll(top, 64, 1), bottom),
        )

    load_src.wait()
    load_prim.wait()

    def lay_out(rp, carry):
        low = pl.ds(pl.multiple_of(rp * 128, 128), 128)
        high = pl.ds(pl.multiple_of(rp * 128 + 2048, 128), 128)
        even, odd = halves(
            src_in[0, :, low].astype(jnp.float32), src_in[0, :, high].astype(jnp.float32)
        )
        source[2 * rp] = even
        source[2 * rp + 1] = odd
        fields = [
            [prim_in[0, k, :, part].astype(jnp.float32) for part in (low, high)] for k in range(3)
        ]
        even, odd = halves(fields[2][0] - fields[1][0], fields[2][1] - fields[1][1])
        diff21[2 * rp] = even
        diff21[2 * rp + 1] = odd
        even, odd = halves(fields[1][0] - fields[0][0], fields[1][1] - fields[0][1])
        diff10[2 * rp] = even
        diff10[2 * rp + 1] = odd
        return carry

    lax.fori_loop(0, 16, lay_out, 0, unroll=4)

    zeros8 = jnp.zeros((34, 8, 128), jnp.float32)
    for buf in (va, vb):
        buf[:, 0:8, :] = zeros8
        buf[:, 56:64, :] = zeros8

    lane_in = lax.broadcasted_iota(jnp.int32, (128, 128), 0)
    lane_out = lax.broadcasted_iota(jnp.int32, (128, 128), 1)
    apart = lane_in - lane_out
    beside = ((apart == 1) | (apart == -1)) & (lane_in // 64 == lane_out // 64)
    beside = jnp.where(beside, 1.0, 0.0).astype(jnp.bfloat16)
    beside = jnp.concatenate([beside, beside], axis=0)

    wait_all(rq)
    onehot = request[...]
    pick = onehot.astype(jnp.bfloat16)
    place = onehot.T.astype(jnp.bfloat16)
    gather_sends = len(sends)
    pk = []
    for p in range(FETCH.count):
        wait_all(ag[p])
        for c in range(FETCH.chunks[p]):
            cells = gathered[p, :, :, c * 128 : (c + 1) * 128].reshape(TILES, 128)
            picked[p, :, c * ENTRIES : (c + 1) * ENTRIES, :] = onehot_dot(pick, cells).reshape(
                NSND, ENTRIES, 128
            )
        rows = FETCH.rows(p, snd)
        size = FETCH.chunks[p] * ENTRIES
        pk.append(
            send_all(
                [(picked.at[p, to, 0:size], returned.at[rows], (to, tile)) for to in column],
                pk_send.at[p],
                pk_recv.at[p],
                returned.at[FETCH.seven(p)],
            )
        )
        returned[rows, :] = picked[p, snd, 0 : FETCH.chunks[p] * ENTRIES]

    drain(gather_sends)

    lane8 = lax.broadcasted_iota(jnp.int32, (8, 128), 1)

    def block_rows(step, g):
        db, rest = step // 4, step % 4
        th, b1 = rest // 2, rest % 2
        entry = (2 * (g // 4) + b1) * 4 + g % 4
        first = (db * 16 + th) * ENTRIES + entry
        return pl.ds(first, 8, stride=2 * ENTRIES), pl.multiple_of(db * 8, 8), b1 * 16 + th * 8

    def enter(step, carry):
        blocks = []
        for g in range(8):
            rows, depth, row = block_rows(step, g)
            blocks.append(returned[rows, :])
        for q, phi in enumerate(exchange_groups(blocks, lane8)):
            smooth = jnp.tanh(phi / front_width)
            cond = jnp.exp(log_low + 0.5 * log_span * (1.0 + smooth))
            at = pl.ds(depth, 8)
            inv = 1.0 / (6.0 + cond)
            conduct[row + q, at, :] = cond
            inverse[row + q, at, :] = inv
            slope[row + q, at, :] = (
                cond * (0.5 * log_span / front_width) * (1.0 - smooth * smooth)
            )
            va[row + q + 1, pl.ds(depth + 8, 8), :] = source[row + q, at, :] * inv
        return carry

    for p in range(FETCH.count):
        wait_all(pk[p])
        lax.fori_loop(*FETCH.steps(p), enter, 0, unroll=min(8, FETCH.depths[p] // 2))

    def sweep(now, keep):
        now[0, 8:56, :] = jnp.where(left, 0.0, pltpu.roll(now[32, 8:56, :], 64, 1))
        now[33, 8:56, :] = jnp.where(left, pltpu.roll(now[1, 8:56, :], 64, 1), 0.0)
        v = now[1:33, 8:56, :].reshape(32 * DEPTH, 128)
        hi = v.astype(jnp.bfloat16)
        lo = (v - hi.astype(jnp.float32)).astype(jnp.bfloat16)
        columns = jnp.dot(
            jnp.concatenate([hi, lo], axis=1), beside, preferred_element_type=jnp.float32
        ).reshape(32, DEPTH, 128)
        for row in range(32):
            total = now[row + 1, 7:55, :] + now[row + 1, 9:57, :]
            total = total + (now[row, 8:56, :] + now[row + 2, 8:56, :])
            total = total + columns[row]
            keep(row, (source[row] + total) * inverse[row])

    def solve(now, later, last):
        def into(buf):
            def keep(row, value):
                buf[row + 1, 8:56, :] = value

            return keep

        def pair(_, carry):
            sweep(now, into(later))
            sweep(later, into(now))
            return carry

        lax.fori_loop(0, (JACOBI - 2) // 2, pair, 0)
        sweep(now, last)

    def between(row, value):
        adjoint_two[row] = value
        rhs = conduct[row] * value
        source[row] = rhs
        vb[row + 1, 8:56, :] = rhs * inverse[row]

    def gradient(row, value):
        va[row + 1, 8:56, :] = -slope[row] * (
            adjoint_two[row] * diff21[row] + value * diff10[row]
        )

    solve(va, vb, between)
    solve(vb, va, gradient)

    def leave(step, carry):
        _, depth, row = block_rows(step, 0)
        blocks = [va[row + q + 1, pl.ds(depth + 8, 8), :] for q in range(8)]
        for g, block in enumerate(exchange_groups(blocks, lane8)):
            rows, _, _ = block_rows(step, g)
            outgoing[rows, :] = block
        return carry

    pick_sends = len(sends)
    og = []
    for p in range(GIVE.count):
        lax.fori_loop(*GIVE.steps(p), leave, 0, unroll=min(8, GIVE.depths[p] // 2))
        size = GIVE.chunks[p] * ENTRIES
        og.append(
            send_all(
                [
                    (outgoing.at[GIVE.rows(p, to)], arrived.at[p, snd, 0:size], (to, tile))
                    for to in column
                ],
                og_send.at[p],
                og_recv.at[p],
                arrived.at[p, 0:7, 0:size],
            )
        )
        rows = GIVE.rows(p, snd)
        arrived[p, snd, 0 : GIVE.chunks[p] * ENTRIES] = outgoing[rows, :]

    drain(pick_sends)

    og_sends = len(sends)
    rs = []
    for p in range(GIVE.count):
        wait_all(og[p])
        for c in range(GIVE.chunks[p]):
            cells = arrived[p, :, c * ENTRIES : (c + 1) * ENTRIES, :].reshape(TILES, 128)
            partial[p, :, :, c * 128 : (c + 1) * 128] = onehot_dot(place, cells).reshape(
                NTILE, TDEV, 128
            )
        rs.append(
            send_all(
                [
                    (partial.at[p, to, :, GIVE.within(p)], owned.at[p, tile, :, GIVE.within(p)], (snd, to))
                    for to in plane
                ],
                rs_send.at[p],
                rs_recv.at[p],
                owned.at[p, 0:15, :, GIVE.within(p)],
            )
        )
        owned[p, tile, :, GIVE.within(p)] = partial[p, tile, :, GIVE.within(p)]

    drain(og_sends)

    rs_sends = len(sends)
    fin = []
    top = jnp.zeros((TDEV, 128), jnp.float32)
    for p in range(GIVE.count):
        wait_all(rs[p])
        slab = owned[p, 0, :, GIVE.within(p)]
        for i in range(1, NTILE):
            slab = slab + owned[p, i, :, GIVE.within(p)]
        cells = GIVE.cells(p, snd)
        grad_ref[:, cells] = slab
        size = jnp.abs(slab)
        for c in range(GIVE.chunks[p]):
            top = jnp.maximum(top, size[:, c * 128 : (c + 1) * 128])
        if p == GIVE.count - 1:
            peaks[tile] = jnp.max(top, axis=0, keepdims=True)
            peak = peaks.at[tile]
            mp = send_all(
                [(peak, peak, (snd, to)) for to in plane],
                mp_send.at[0],
                mp_recv.at[0],
                peaks.at[0:15],
            )
        block = grad_ref.at[:, cells]
        fin.append(
            send_all(
                [(block, block, (to, tile)) for to in column],
                fin_send.at[p],
                fin_recv.at[p],
                grad_ref.at[:, pl.ds(0, 7 * GIVE.chunks[p] * 128)],
            )
        )

    drain(rs_sends)

    wait_all(mp)
    peaks2[snd] = jnp.max(peaks[...], axis=0)
    peak = peaks2.at[snd]
    mc = send_all(
        [(peak, peak, (to, tile)) for to in column], mc_send.at[0], mc_recv.at[0], peaks2.at[0:7]
    )
    drain(len(sends) - 1)
    for pair in fin:
        wait_all(pair)
    store = pltpu.make_async_copy(grad_ref, grad_out, local_sem.at[0])
    store.start()
    wait_all(mc)
    peak_ref[...] = jnp.broadcast_to(jnp.max(peaks2[...], axis=0), (8, 128))
    drain(len(sends))
    store.wait()


def finish(grad, peak, level_set, grad_out, next_out, grad_in, peak_in, level_in, blank, sem):
    rest = level_set.shape[1] - TOP
    head, tail = pl.ds(0, TOP), pl.ds(TOP, rest)

    def copy(i, src, dst):
        c = pltpu.make_async_copy(src, dst, sem.at[i])
        c.start()
        return c

    reads = [
        copy(0, level_set.at[:, tail], level_in.at[:, tail]),
        copy(1, peak, peak_in),
        copy(2, grad, grad_in),
        copy(3, level_set.at[:, head], level_in.at[:, head]),
    ]
    blank[...] = jnp.zeros((TDEV, rest), jnp.float32)
    writes = [copy(4, blank, grad_out.at[:, tail])]
    reads[0].wait()
    writes.append(copy(5, level_in.at[:, tail], next_out.at[:, tail]))
    for c in reads[1:3]:
        c.wait()
    writes.append(copy(6, grad_in, grad_out.at[:, head]))
    scale = step_size / (jnp.max(peak_in[...]) + 1e-6)
    reads[3].wait()
    level_in[:, head] = level_in[:, head] - scale * grad_in[...]
    writes.append(copy(7, level_in.at[:, head], next_out.at[:, head]))
    for c in writes:
        c.wait()


def shards(level_set, tile_home, footprints, adjoint_source, primal_fields):
    f32 = jnp.float32
    smem = pl.BlockSpec(memory_space=pltpu.SMEM)
    anywhere = pl.BlockSpec(memory_space=pltpu.HBM)
    vmem = pl.BlockSpec(memory_space=pltpu.VMEM)
    field = pltpu.VMEM((32, DEPTH, 128), f32)
    padded = pltpu.VMEM((34, DEPTH + 16, 128), f32)
    dma = pltpu.SemaphoreType.DMA
    grad, peak = pl.pallas_call(
        kernel,
        out_shape=(
            jax.ShapeDtypeStruct((TDEV, TOP), f32),
            jax.ShapeDtypeStruct((8, 128), f32),
        ),
        in_specs=[smem, smem, anywhere, anywhere, anywhere],
        out_specs=(anywhere, vmem),
        scratch_shapes=[
            pltpu.VMEM(adjoint_source.shape, jnp.bfloat16),
            pltpu.VMEM(primal_fields.shape, jnp.bfloat16),
            pltpu.VMEM((FETCH.count, NTILE, TDEV, FETCH.most * 128), f32),
            pltpu.VMEM((NSND * ENTRIES, TILES), f32),
            pltpu.VMEM((FETCH.count, NSND, FETCH.most * ENTRIES, 128), f32),
            pltpu.VMEM((NSND * SROWS, 128), f32),
            field,
            field,
            field,
            field,
            field,
            field,
            padded,
            padded,
            field,
            pltpu.VMEM((NSND * SROWS, 128), f32),
            pltpu.VMEM((GIVE.count, NSND, GIVE.most * ENTRIES, 128), f32),
            pltpu.VMEM((GIVE.count, NTILE, TDEV, GIVE.most * 128), f32),
            pltpu.VMEM((GIVE.count, NTILE, TDEV, GIVE.most * 128), f32),
            pltpu.VMEM((NTILE, 1, 128), f32),
            pltpu.VMEM((NSND, 1, 128), f32),
            pltpu.VMEM((TDEV, TOP), f32),
            dma((FETCH.count + 2,)),
            dma((FETCH.count,)),
            dma((FETCH.count,)),
            dma((FETCH.count,)),
            dma((FETCH.count,)),
            dma((FETCH.count,)),
            dma((FETCH.count,)),
            dma((GIVE.count,)),
            dma((GIVE.count,)),
            dma((GIVE.count,)),
            dma((GIVE.count,)),
            dma((GIVE.count,)),
            dma((GIVE.count,)),
            dma((GIVE.count,)),
            dma((GIVE.count,)),
            dma((GIVE.count,)),
            dma((GIVE.count,)),
        ],
        compiler_params=pltpu.CompilerParams(
            collective_id=0, has_side_effects=True, vmem_limit_bytes=VMEM_LIMIT
        ),
    )(footprints, tile_home, level_set, adjoint_source, primal_fields)
    out = jax.ShapeDtypeStruct(level_set.shape, f32)
    return pl.pallas_call(
        finish,
        out_shape=(out, out),
        in_specs=[anywhere, anywhere, anywhere],
        out_specs=(anywhere, anywhere),
        scratch_shapes=[
            pltpu.VMEM((TDEV, TOP), f32),
            pltpu.VMEM((8, 128), f32),
            pltpu.VMEM(level_set.shape, f32),
            pltpu.VMEM((TDEV, level_set.shape[1] - TOP), f32),
            dma((8,)),
        ],
        compiler_params=pltpu.CompilerParams(vmem_limit_bytes=VMEM_LIMIT),
    )(grad, peak, level_set)


def solution(mesh):
    return jax.shard_map(
        shards,
        mesh=mesh,
        in_specs=(
            P("tile", None),
            P(),
            P(("snd", "tile"), None),
            P(("snd", "tile"), None, None),
            P(("snd", "tile"), None, None, None),
        ),
        out_specs=(P("tile", None), P("tile", None)),
        check_vma=False,
    )
```
